128 devices in a mesh: dp: 16 (over x_hi, y, core), frame: 8 (over z, x_lo).
Axes of the slice: x: 4 (x_hi: 2, x_lo: 2; x = x_hi * 2 + x_lo), y: 4, z: 4, core: 2. Of those that a mesh axis runs over, the one named last changes fastest.
Arguments:
- clips_in: bfloat16 [16, 8, 8, 96, 640], P('dp', 'frame'), may hold values from -40 to 40
- teacher: bfloat16 [16, 8, 8, 96, 640], P('dp', 'frame'), may hold values from -6 to 6
- spatial_weight: bfloat16 [3, 3, 640, 640], replicated, may hold values from -0.078125 to 0.078125
- temporal_weight: bfloat16 [3, 640, 640], replicated, may hold values from -0.125 to 0.125
- norm_gain: float32 [640], replicated, may hold values from 0.5 to 1.5
- norm_bias: float32 [640], replicated, may hold values from -3 to 3
Outputs:
- spatial_grad: float32 [5760, 640], P(('dp', 'frame'))
- temporal_grad: float32 [1920, 640], P(('dp', 'frame'))
- gain_grad: float32 [640], replicated
- bias_grad: float32 [640], replicated
- loss: float32 [], replicated
The draws below stay inside these ranges and needn't reach their ends.
All inputs are finite; a program needn't handle non-finite values.
Results may differ from the reference program's by a relative error of at most 0.0045.
Values may be sent and summed in bfloat16 or wider, within the bound.
A program may use at most 128 MiB of HBM per device.

```python
import jax
import jax.numpy as jnp
from jax import lax

C = 640
GROUPS = 32
H = 8
W = 96
CLIPS = 16
FRAMES = 8


def draw_clips_in(key, part):
    key = jax.random.fold_in(key, 11)
    subkeys = jax.random.split(key, 3)
    full_shape = (CLIPS, FRAMES, H, W, C)
    frame_ramp = 3.0 ** (jnp.arange(FRAMES, dtype=jnp.float32) / max(FRAMES - 1, 1))
    spread = jnp.exp(jax.random.uniform(subkeys[1], (C,), jnp.float32, jnp.log(0.3), jnp.log(3.0)))
    offset = 0.5 * jnp.clip(jax.random.normal(subkeys[2], (C,), jnp.float32), -4.0, 4.0)
    draws_base = jnp.clip(jax.random.normal(subkeys[0], full_shape, jnp.float32), -6.0, 6.0)
    values = (draws_base * spread + offset) * frame_ramp[None, :, None, None, None]
    return jnp.clip(values, -40.0, 40.0).astype(jnp.bfloat16)


def steps_of(own_key, extent, shards, smallest, largest):
    level, own = 1.0, jax.random.fold_in(own_key, 6)
    for position, shards_of in shards:
        draws = jnp.exp(jax.random.uniform(jax.random.fold_in(own, position), (shards_of,), jnp.float32, smallest / len(shards), largest / len(shards)))
        level = level * jnp.repeat(draws, extent[position] // shards_of).reshape([-1 if axis == position else 1 for axis in range(len(extent))])
    return level


def normal_values(stream_key, extent, scale, reach, pieces=(), kind=jnp.bfloat16):
    values = jax.random.normal(stream_key, extent, jnp.float32) * scale
    if len(pieces) > 0:
        values = steps_of(stream_key, extent, pieces, -0.22, 0.18) * values
    return jnp.clip(values, min=-reach, max=reach).astype(kind)


def setup_inputs(seed: int = 0) -> dict:
    keys = jax.random.split(jax.random.key(seed), 7)
    return {
        "clips_in": draw_clips_in(jax.random.fold_in(keys[6], 71), 0),
        "teacher": normal_values(keys[1], (CLIPS, FRAMES, H, W, C), 1.0, 6.0, ((0, 16), (1, 8))),
        "spatial_weight": normal_values(keys[2], (3, 3, C, C), (9 * C) ** -0.5, 0.078125),
        "temporal_weight": normal_values(keys[3], (3, C, C), (3 * C) ** -0.5, 0.125),
        "norm_gain": jnp.clip(1.0 + 0.1 * jax.random.normal(keys[4], (C,), jnp.float32), 0.5, 1.5),
        "norm_bias": normal_values(keys[5], (C,), 0.5, 3.0, (), jnp.float32),
    }


EPSILON = 1e-05

def group_moments(video, groups):
    floats = video.astype(jnp.float32)
    sums = lax.optimization_barrier(jnp.sum(floats, axis=(1, 2, 3)))
    squares = lax.optimization_barrier(jnp.sum(floats * floats, axis=(1, 2, 3)))
    batch = sums.shape[0]
    return (sums.reshape(batch, groups, -1).sum(-1), squares.reshape(batch, groups, -1).sum(-1))

def normalize(video, gain, shift_term, sums, squares, group_size):
    channels = video.shape[-1]
    group_mean = sums / group_size
    variance = squares / group_size - group_mean * group_mean
    inverse = lax.rsqrt(variance + EPSILON)
    repeat_by = channels // sums.shape[1]
    mean_wide = jnp.repeat(group_mean, repeat_by, axis=1)[:, None, None, None, :]
    scale_wide = jnp.repeat(inverse, repeat_by, axis=1)[:, None, None, None, :]
    centred = (video.astype(jnp.float32) - mean_wide) * scale_wide
    return (centred, centred * gain + shift_term)

def spatial_forward(hidden, weights):
    span_rows, span_cols, channels = (hidden.shape[2], hidden.shape[3], hidden.shape[4])
    padded = jnp.pad(hidden, ((0, 0), (0, 0), (1, 1), (1, 1), (0, 0)))
    running = jnp.zeros((hidden.size // channels, channels), jnp.float32)
    for row_tap in range(3):
        for col_tap in range(3):
            window = padded[:, :, row_tap:row_tap + span_rows, col_tap:col_tap + span_cols, :].reshape(-1, channels)
            running = running + jnp.dot(window, weights[row_tap, col_tap], preferred_element_type=jnp.float32)
    return running

def spatial_backward(grad_state, hidden, weights):
    span_rows, span_cols, channels = (hidden.shape[2], hidden.shape[3], hidden.shape[4])
    grad_pad = jnp.pad(grad_state, ((0, 0), (0, 0), (1, 1), (1, 1), (0, 0)))
    hidden_pad = jnp.pad(hidden, ((0, 0), (0, 0), (1, 1), (1, 1), (0, 0)))
    center = grad_state.reshape(-1, channels)
    running = jnp.zeros((hidden.size // channels, channels), jnp.float32)
    tap_grads = []
    for row_tap in range(3):
        for col_tap in range(3):
            window = grad_pad[:, :, 2 - row_tap:2 - row_tap + span_rows, 2 - col_tap:2 - col_tap + span_cols, :].reshape(-1, channels)
            running = running + lax.dot_general(window, weights[row_tap, col_tap], (((1,), (1,)), ((), ())), preferred_element_type=jnp.float32)
            source = hidden_pad[:, :, row_tap:row_tap + span_rows, col_tap:col_tap + span_cols, :].reshape(-1, channels)
            tap_grads.append(lax.dot_general(source, center, (((0,), (0,)), ((), ())), preferred_element_type=jnp.float32))
    return (running, jnp.stack(tap_grads).reshape(3, 3, channels, channels))

def temporal_forward(padded, weights, frames_count):
    channels = padded.shape[-1]
    running = jnp.zeros((padded.shape[0] * frames_count * padded.shape[2], channels), jnp.float32)
    for tap in range(3):
        window = padded[:, tap:tap + frames_count].reshape(-1, channels)
        running = running + jnp.dot(window, weights[tap], preferred_element_type=jnp.float32)
    return running

def temporal_backward(grad_pad, state_pad, weights, frames_count):
    channels = grad_pad.shape[-1]
    center = grad_pad[:, 1:1 + frames_count].reshape(-1, channels)
    running = jnp.zeros(center.shape, jnp.float32)
    tap_grads = []
    for tap in range(3):
        window = grad_pad[:, 2 - tap:2 - tap + frames_count].reshape(-1, channels)
        running = running + lax.dot_general(window, weights[tap], (((1,), (1,)), ((), ())), preferred_element_type=jnp.float32)
        source = state_pad[:, tap:tap + frames_count].reshape(-1, channels)
        tap_grads.append(lax.dot_general(source, center, (((0,), (0,)), ((), ())), preferred_element_type=jnp.float32))
    return (running, jnp.stack(tap_grads))

def reference(clips_in, teacher, spatial_weight, temporal_weight, norm_gain, norm_bias):
    grad_scale = float(CLIPS * FRAMES * H * W) ** (-0.5)
    group_size = FRAMES * H * W * (C // GROUPS)

    def clip_pass(carry, pair):
        video = pair[0][None]
        target = pair[1][None]
        sums, squares = group_moments(video, GROUPS)
        centred, normed = normalize(video, norm_gain, norm_bias, sums, squares, group_size)
        hidden = jax.nn.silu(normed).astype(jnp.bfloat16)
        spatial_out = spatial_forward(hidden, spatial_weight).astype(jnp.bfloat16).reshape(1, FRAMES, H * W, C)
        state_pad = jnp.pad(spatial_out, ((0, 0), (1, 1), (0, 0), (0, 0)))
        temporal_out = temporal_forward(state_pad, temporal_weight, FRAMES).astype(jnp.bfloat16).reshape(1, FRAMES, H * W, C)
        error = video.reshape(1, FRAMES, H * W, C).astype(jnp.float32) + temporal_out.astype(jnp.float32) - target.reshape(1, FRAMES, H * W, C).astype(jnp.float32)
        grad_out = (error * grad_scale).astype(jnp.bfloat16)
        grad_pad = jnp.pad(grad_out, ((0, 0), (1, 1), (0, 0), (0, 0)))
        grad_state, time_grad = temporal_backward(grad_pad, state_pad, temporal_weight, FRAMES)
        grad_state = grad_state.astype(jnp.bfloat16).reshape(1, FRAMES, H, W, C)
        grad_hidden, space_grad = spatial_backward(grad_state, hidden, spatial_weight)
        grad_hidden = grad_hidden.reshape(1, FRAMES, H, W, C)
        sigmoid = jax.nn.sigmoid(normed)
        grad_norm = grad_hidden * sigmoid * (1.0 + normed * (1.0 - sigmoid))
        gain_part = lax.optimization_barrier(jnp.sum(grad_norm * centred, axis=(0, 1, 2, 3)))
        bias_part = lax.optimization_barrier(jnp.sum(grad_norm, axis=(0, 1, 2, 3)))
        squared = jnp.sum(error * error)
        return ((carry[0] + space_grad, carry[1] + time_grad, carry[2] + gain_part, carry[3] + bias_part, carry[4] + squared), None)
    start = (jnp.zeros((3, 3, C, C), jnp.float32), jnp.zeros((3, C, C), jnp.float32), jnp.zeros((C,), jnp.float32), jnp.zeros((C,), jnp.float32), jnp.zeros((), jnp.float32))
    totals, unused = lax.scan(clip_pass, start, (clips_in, teacher))
    loss = totals[4] / float(CLIPS * FRAMES * H * W * C)
    return (totals[0].reshape(9 * C, C), totals[1].reshape(3 * C, C), totals[2], totals[3], loss)
```

```python
import jax
import jax.numpy as jnp
from jax import lax
from jax.experimental import pallas as pl
from jax.experimental.pallas import tpu as pltpu
from jax.sharding import PartitionSpec as P

GROUPS = 32
EPSILON = 1e-05
F32 = jnp.float32
BF16 = jnp.bfloat16
MESH = pl.DeviceIdType.MESH

FRAMES = 8
ROWS = 8
COLS = 96
C = 640
OWN = COLS // FRAMES
WIDE = OWN + 2
CELLS = OWN * FRAMES * ROWS
CELLS_WIDE = WIDE * FRAMES * ROWS
SLAB = FRAMES * ROWS
BLOCK = 16
ORDERS = ((2, 0, 1), (1, 2, 0), (0, 1, 2), (1, 2, 0))


def rem(a, b):
    return lax.rem(a, jnp.int32(b))


def div(a, b):
    return lax.div(a, jnp.int32(b))


class Place:
    def __init__(self):
        self.dp = lax.axis_index("dp")
        self.fr = lax.axis_index("frame")
        self.core = rem(self.dp, 2)
        self.y = rem(div(self.dp, 2), 4)
        self.xh = div(self.dp, 8)
        self.z = div(self.fr, 2)
        self.xl = rem(self.fr, 2)
        self.x = 2 * self.xh + self.xl
        self.group = self.xh * 4 + self.y
        self.along = (self.x, self.y, self.z)

    def device(self, x, y, z):
        return (div(x, 2) * 8 + y * 2 + self.core, z * 2 + rem(x, 2))

    def peer(self, axis, step):
        there = rem(self.along[axis] + step, 4)
        at = [self.x, self.y, self.z]
        at[axis] = there
        return there, self.device(*at)


def kernel(
    xs, ts, gain_ref, bias_ref, w_hbm, wt_hbm,
    rows_out, small_out,
    w, wt, xr, tr, stats, hid, hid_t, hid_p, s3, s3_t, s3_p, g3, go, gs, xj, acc,
    stage, r1, p2, r2, p3, r3, fin, small_a, small_b,
    w_sem, own_sem, x_send, x_recv, t_send, t_recv, st_send, st_recv, pair_send, pair_recv,
    r1_send, r1_recv, r2_send, r2_recv, r3_send, r3_recv, fix_send, fix_recv,
    a_send, a_recv, b_send, b_recv,
):
    me = Place()
    dp, fr, core = me.dp, me.fr, me.core
    gs3 = s3

    w_copies = []
    for a in range(3):
        for c in range(3):
            w_copies.append(
                pltpu.make_async_copy(
                    w_hbm.at[a, c], w.at[c, pl.ds(a * C, C)], w_sem.at[3 * a + c]
                )
            )
    w_copies.append(pltpu.make_async_copy(wt_hbm, wt, w_sem.at[9]))
    for copy in w_copies:
        copy.start()

    barrier = pltpu.get_barrier_semaphore()
    for s in range(1, 8):
        pl.semaphore_signal(
            barrier, inc=1, device_id=(dp, rem(fr + s, 8)), device_id_type=MESH
        )
    for s in range(1, 16):
        pl.semaphore_signal(
            barrier, inc=1, device_id=(rem(dp + s, 16), fr), device_id_type=MESH
        )
    pl.semaphore_signal(
        barrier, inc=1, device_id=(rem(dp + 8, 16), fr + 1 - 2 * me.xl), device_id_type=MESH
    )
    partner = (dp + 1 - 2 * core, fr)

    @pl.when(fr == 0)
    def _():
        pl.semaphore_signal(
            barrier, inc=1, device_id=(dp + 1 - 2 * core, 7), device_id_type=MESH
        )

    own_x = pltpu.make_async_copy(xs.at[fr], xr.at[fr], own_sem.at[0])
    own_x.start()
    own_t = pltpu.make_async_copy(ts.at[fr], tr.at[fr], own_sem.at[1])
    own_t.start()

    def moment_body(d, carry):
        total, square = carry
        v = xs[d].astype(F32)[ROWS : ROWS + OWN * ROWS]
        v = v.reshape(OWN, ROWS, C)
        return (total + jnp.sum(v, axis=0), square + jnp.sum(v * v, axis=0))

    zero = jnp.zeros((ROWS, C), F32)
    total, square = lax.fori_loop(0, FRAMES, moment_body, (zero, zero))
    stats[fr, 0:8] = total
    stats[fr, 8:16] = square

    pl.semaphore_wait(barrier, 23 + (fr == 7).astype(jnp.int32))

    sends = []
    for s in range(1, 8):
        to = rem(fr + s, 8)
        copy = pltpu.make_async_remote_copy(
            stats.at[fr], stats.at[fr], st_send.at[s], st_recv.at[s],
            device_id=(dp, to), device_id_type=MESH,
        )
        copy.start()
        sends.append(copy)
    for s in range(1, 8):
        to = rem(fr + s, 8)
        copy = pltpu.make_async_remote_copy(
            xs.at[to], xr.at[fr], x_send.at[s], x_recv.at[s],
            device_id=(dp, to), device_id_type=MESH,
        )
        copy.start()
        sends.append(copy)
    for s in range(1, 8):
        to = rem(fr + s, 8)
        copy = pltpu.make_async_remote_copy(
            ts.at[to], tr.at[fr], t_send.at[s], t_recv.at[s],
            device_id=(dp, to), device_id_type=MESH,
        )
        copy.start()
        sends.append(copy)

    hid_t[9 * C :, :] = jnp.zeros((48, CELLS), BF16)
    s3_t[3 * C :, :] = jnp.zeros((16, CELLS), BF16)

    row = lax.broadcasted_iota(jnp.int32, (C, C), 0)
    col = lax.broadcasted_iota(jnp.int32, (C, C), 1)
    same = (
        lax.shift_right_logical(row * 3277, 16) == lax.shift_right_logical(col * 3277, 16)
    ).astype(F32)
    for s in range(1, 8):
        sender = rem(fr - s + 8, 8)
        pltpu.make_async_remote_copy(
            stats.at[sender], stats.at[sender], st_send.at[s], st_recv.at[s],
            device_id=(dp, sender), device_id_type=MESH,
        ).wait_recv()
    moments = stats[0]
    for f in range(1, FRAMES):
        moments = moments + stats[f]
    wide = jnp.dot(moments, same, precision=lax.Precision.HIGHEST, preferred_element_type=F32)
    size = float(FRAMES * ROWS * COLS * (C // GROUPS))
    mean = jnp.sum(wide[0:8], axis=0, keepdims=True) / size
    variance = jnp.sum(wide[8:16], axis=0, keepdims=True) / size - mean * mean
    inverse = lax.rsqrt(variance + EPSILON)
    gain = gain_ref[...]
    bias = bias_ref[...]

    own_x.wait()
    for s in range(1, 8):
        sender = rem(fr - s + 8, 8)
        pltpu.make_async_remote_copy(
            xr.at[sender], xr.at[sender], x_send.at[s], x_recv.at[s],
            device_id=(dp, sender), device_id_type=MESH,
        ).wait_recv()

    cell_row = rem(lax.broadcasted_iota(jnp.int32, (BLOCK, C), 0), 8)

    def valid_of(j):
        outside = ((j == 0) & (fr == 0)) | ((j == WIDE - 1) & (fr == FRAMES - 1))
        return 1.0 - outside.astype(F32)

    def sigmoid(v):
        return 0.5 * jnp.tanh(0.5 * v) + 0.5

    def store_row_shifts(ref, at, value, first, last):
        ref[at, first * C : (first + 1) * C] = jnp.where(
            cell_row == 0, 0.0, pltpu.roll(value, 1, 0)
        ).astype(BF16)
        ref[at, C : 2 * C] = value.astype(BF16)
        ref[at, last * C : (last + 1) * C] = jnp.where(
            cell_row == 7, 0.0, pltpu.roll(value, BLOCK - 1, 0)
        ).astype(BF16)

    def hidden_body(n, carry):
        p = div(n, WIDE // 2)
        jj = rem(n, WIDE // 2)
        at = pl.ds(pl.multiple_of(jj * 16, 16), 16)
        even = xr[2 * p, at].astype(F32)
        odd = xr[2 * p + 1, at].astype(F32)
        for h in range(2):
            j = 2 * jj + h
            v = jnp.concatenate([even[8 * h : 8 * h + 8], odd[8 * h : 8 * h + 8]], axis=0)
            normed = (v - mean) * inverse * gain + bias
            value = normed * sigmoid(normed) * valid_of(j)
            dst = pl.ds(pl.multiple_of(j * SLAB + p * 16, 16), 16)
            xj[dst, :] = v.astype(BF16)
            store_row_shifts(hid, dst, value, 0, 2)
        return carry

    lax.fori_loop(0, 4 * (WIDE // 2), hidden_body, 0)

    def transpose_body(n, carry):
        c = div(n, 6)
        b = rem(n, 6)
        src = pl.ds(pl.multiple_of(c * SLAB + b * 128, 64), 128)
        for a in range(3):
            dst = pl.ds(pl.multiple_of((a * 3 + c) * C, 128), C)
            hid_t[dst, pl.ds(pl.multiple_of(b * 128, 128), 128)] = hid[
                src, a * C : (a + 1) * C
            ].T
        return carry

    lax.fori_loop(0, 18, transpose_body, 0)

    def pair_copy(src, dst, n):
        return pltpu.make_async_remote_copy(
            src, dst, pair_send.at[n], pair_recv.at[n], device_id=partner, device_id_type=MESH
        )

    for m in range(8):
        src = pl.ds(pl.multiple_of(720 * m + 384 * (1 - core), 16), 384)
        pair_copy(hid_t.at[src], hid_p.at[m], 0).start()

    for copy in w_copies:
        copy.wait()

    def conv_body(b, carry):
        total = None
        for c in range(3):
            src = pl.ds(pl.multiple_of(b * 256 + c * SLAB, 64), 256)
            part = jnp.dot(hid[src, :], w[c], preferred_element_type=F32)
            total = part if total is None else total + part
        acc[pl.ds(pl.multiple_of(b * 256, 256), 256), :] = total
        return carry

    lax.fori_loop(0, 3, conv_body, 0)

    pad8 = jnp.zeros((8, C), F32)

    def store_frame_shifts(ref, at, value, before, after):
        ref[at, before * C : (before + 1) * C] = jnp.concatenate(
            [pad8, value[: SLAB - 8]], axis=0
        ).astype(BF16)
        ref[at, C : 2 * C] = value.astype(BF16)
        ref[at, after * C : (after + 1) * C] = jnp.concatenate(
            [value[8:], pad8], axis=0
        ).astype(BF16)

    def state_body(j, carry):
        at = pl.ds(pl.multiple_of(j * SLAB, SLAB), SLAB)
        store_frame_shifts(s3, at, acc[at, :], 0, 2)
        return carry

    lax.fori_loop(0, OWN, state_body, 0)

    def temporal_body(b, carry):
        src = pl.ds(pl.multiple_of(b * 256, 256), 256)
        acc[src, :] = jnp.dot(s3[src, :], wt[...], preferred_element_type=F32)
        return carry

    lax.fori_loop(0, 3, temporal_body, 0)

    own_t.wait()
    for s in range(1, 8):
        sender = rem(fr - s + 8, 8)
        pltpu.make_async_remote_copy(
            tr.at[sender], tr.at[sender], t_send.at[s], t_recv.at[s],
            device_id=(dp, sender), device_id_type=MESH,
        ).wait_recv()

    scale = float(16 * FRAMES * ROWS * COLS) ** (-0.5)

    def error_body(jj, loss):
        at = pl.ds(pl.multiple_of(jj * 16, 16), 16)
        target = [tr[f, at].astype(F32) for f in range(FRAMES)]
        for h in range(2):
            j = 2 * jj + h
            own = pl.ds(pl.multiple_of(j * SLAB, SLAB), SLAB)
            wide_at = pl.ds(pl.multiple_of((j + 1) * SLAB, SLAB), SLAB)
            taught = jnp.concatenate([t[8 * h : 8 * h + 8] for t in target], axis=0)
            out = acc[own, :].astype(BF16).astype(F32)
            error = xj[wide_at, :].astype(F32) + out - taught
            grad = error * scale
            go[0, own, :] = grad.astype(BF16)
            store_frame_shifts(g3, own, grad, 2, 0)
            loss = loss + jnp.sum((error * error).reshape(FRAMES, 8, C), axis=0)
        return loss

    loss = lax.fori_loop(0, OWN // 2, error_body, jnp.zeros((8, C), F32))
    pair_copy(go.at[0], go.at[1], 1).start()

    def state_transpose_body(b, carry):
        src = pl.ds(pl.multiple_of(b * 128, 128), 128)
        for t in range(3):
            s3_t[t * C : (t + 1) * C, src] = s3[src, t * C : (t + 1) * C].T
        return carry

    lax.fori_loop(0, 6, state_transpose_body, 0)
    for m in range(8):
        src = pl.ds(pl.multiple_of(240 * m + 128 * (1 - core), 16), 128)
        pair_copy(s3_t.at[src], s3_p.at[m], 2).start()

    def nt(lhs, rhs):
        return lax.dot_general(lhs, rhs, (((1,), (1,)), ((), ())), preferred_element_type=F32)

    def state_grad_body(b, carry):
        src = pl.ds(pl.multiple_of(b * 256, 256), 256)
        total = None
        for t in range(3):
            part = nt(g3[src, t * C : (t + 1) * C], wt[t * C : (t + 1) * C, :])
            total = part if total is None else total + part
        acc[src, :] = total
        return carry

    lax.fori_loop(0, 3, state_grad_body, 0)

    def grad_state_body(b, carry):
        at = pl.ds(pl.multiple_of(b * 16, 16), 16)
        value = acc[at, :]
        gs[0, at, :] = value.astype(BF16)
        store_row_shifts(gs3, at, value, 2, 0)
        return carry

    lax.fori_loop(0, CELLS // 16, grad_state_body, 0)
    pair_copy(gs.at[0], gs.at[1], 3).start()

    def wait_pair(dst, n):
        pair_copy(dst, dst, n).wait_recv()

    wait_pair(go.at[1], 1)
    wait_pair(s3_p, 2)

    def time_body(n, carry):
        own = jnp.concatenate(
            [
                s3_t[pl.ds(pl.multiple_of(240 * (4 * n + k) + 128 * core, 16), 128), :]
                for k in range(4)
            ],
            axis=0,
        )
        other = s3_p[pl.ds(4 * n, 4)].reshape(512, CELLS)
        out = jnp.dot(own, go[0], preferred_element_type=F32)
        out = out + jnp.dot(other, go[1], preferred_element_type=F32)
        stage[3, pl.ds(4 * n, 4)] = out.astype(BF16).reshape(4, 8, BLOCK, C)
        return carry

    lax.fori_loop(0, 2, time_body, 0)

    def first_send(u, src, axis, step, dst, device):
        pltpu.make_async_remote_copy(
            src, dst, r1_send.at[u, step - 1], r1_recv.at[u, step - 1],
            device_id=device, device_id_type=MESH,
        ).start()

    def send_y(u, m):
        mx, my = div(m, 4), rem(m, 4)
        step = rem(my - me.y + 4, 4)

        @pl.when(step != 0)
        def _():
            first_send(
                u, stage.at[u, m], 1, step,
                r1.at[u, step - 1, pl.ds(mx * 8, 8)], me.device(me.x, my, me.z),
            )

    def send_z(u, m):
        for s in range(1, 4):
            there, device = me.peer(2, s)
            first_send(
                u, stage.at[u, m, pl.ds(there * 2, 2)], 2, s,
                r1.at[u, s - 1, pl.ds(m * 2, 2)], device,
            )

    def send_x(u, m):
        mx, my = div(m, 4), rem(m, 4)
        for xl in range(2):
            there = 2 * mx + xl
            step = rem(there - me.x + 4, 4)

            @pl.when(step != 0)
            def _():
                first_send(
                    u, stage.at[u, m, pl.ds(xl * 4, 4)], 0, step,
                    r1.at[u, step - 1, pl.ds(my * 4, 4)], me.device(there, me.y, me.z),
                )

    def time_send(n, carry):
        send_y(3, rem(me.group + 1 + n, 8))
        return carry

    lax.fori_loop(0, 8, time_send, 0)

    wait_pair(gs.at[1], 3)
    wait_pair(hid_p, 0)

    def space_body(n, carry):
        m = rem(me.group + 1 + n, 8)
        own = hid_t[pl.ds(pl.multiple_of(720 * m + 384 * core, 16), 384), :]
        out = jnp.dot(own, gs[0], preferred_element_type=F32)
        out = out + jnp.dot(hid_p[m], gs[1], preferred_element_type=F32)
        out = out.astype(BF16)
        for q in range(8):
            zz, xl = q // 2, q % 2
            stage[0, m, q] = out[48 * q : 48 * q + 16]
            stage[1, m, q] = out[48 * q + 16 : 48 * q + 32]
            stage[2, m, xl * 4 + zz] = out[48 * q + 32 : 48 * q + 48]
        send_z(0, m)
        send_y(1, m)
        send_x(2, m)
        return carry

    lax.fori_loop(0, 8, space_body, 0)

    def clear_body(b, carry):
        acc[pl.ds(pl.multiple_of(b * SLAB, SLAB), SLAB), :] = jnp.zeros((SLAB, C), F32)
        return carry

    lax.fori_loop(0, WIDE, clear_body, 0)

    def grad_hidden(c):
        def body(b, carry):
            src = pl.ds(pl.multiple_of(b * 256, 256), 256)
            dst = pl.ds(pl.multiple_of(b * 256 + c * SLAB, 64), 256)
            total = acc[dst, :]
            for a in range(3):
                total = total + nt(gs3[src, a * C : (a + 1) * C], w[c, a * C : (a + 1) * C, :])
            acc[dst, :] = total
            return carry

        lax.fori_loop(0, 3, body, 0)

    def wait_steps(u, buffer, send_sems, recv_sems):
        for s in range(1, 4):
            there, device = me.peer(0, s)
            copy = pltpu.make_async_remote_copy(
                buffer.at[u, s - 1], buffer.at[u, s - 1],
                send_sems.at[u, s - 1], recv_sems.at[u, s - 1],
                device_id=device, device_id_type=MESH,
            )
            copy.wait_recv()

    def wait_sent(u, buffer, send_sems, recv_sems):
        for s in range(1, 4):
            there, device = me.peer(0, s)
            pltpu.make_async_remote_copy(
                buffer.at[u, s - 1], buffer.at[u, s - 1],
                send_sems.at[u, s - 1], recv_sems.at[u, s - 1],
                device_id=device, device_id_type=MESH,
            ).wait_send()

    def second_phase(u):
        wait_steps(u, r1, r1_send, r1_recv)

        def body(k, carry):
            if u == 0:
                m, xl = div(k, 2), rem(k, 2)
                own = stage[0, m, 2 * me.z + xl]
                to = (2 * div(m, 4) + xl) * 4 + rem(m, 4)
            elif u == 2:
                own = stage[2, me.xh * 4 + div(k, 4), me.xl * 4 + rem(k, 4)]
                to = k
            else:
                mx, q = div(k, 8), rem(k, 8)
                own = stage[u, mx * 4 + me.y, q]
                to = div(q, 2) * 4 + mx * 2 + rem(q, 2)
            total = own.astype(F32)
            for s in range(3):
                total = total + r1[u, s, k].astype(F32)
            p2[u, to] = total.astype(BF16)
            return carry

        lax.fori_loop(0, 16, body, 0)
        for s in range(1, 4):
            there, device = me.peer(ORDERS[u][1], s)
            pltpu.make_async_remote_copy(
                p2.at[u, pl.ds(there * 4, 4)], r2.at[u, s - 1],
                r2_send.at[u, s - 1], r2_recv.at[u, s - 1],
                device_id=device, device_id_type=MESH,
            ).start()

    def third_phase(u):
        wait_steps(u, r2, r2_send, r2_recv)
        base = me.along[ORDERS[u][1]] * 4
        for k in range(4):
            total = p2[u, base + k].astype(F32)
            for s in range(3):
                total = total + r2[u, s, k].astype(F32)
            p3[u, k] = total
        for s in range(1, 4):
            there, device = me.peer(ORDERS[u][2], s)
            pltpu.make_async_remote_copy(
                p3.at[u, there], r3.at[u, s - 1],
                r3_send.at[u, s - 1], r3_recv.at[u, s - 1],
                device_id=device, device_id_type=MESH,
            ).start()

    def last_phase(u):
        wait_steps(u, r3, r3_send, r3_recv)
        total = p3[u, me.along[ORDERS[u][2]]]
        for s in range(3):
            total = total + r3[u, s]
        fin[0, u * BLOCK : (u + 1) * BLOCK] = total

    second_phase(3)
    grad_hidden(0)
    third_phase(3)
    for u in range(3):
        second_phase(u)
    grad_hidden(1)
    for u in range(3):
        third_phase(u)
    grad_hidden(2)
    for u in range(4):
        last_phase(u)

    last = (fr == 7).astype(jnp.int32)
    nxt = (dp + last * (1 - 2 * core), rem(fr + 1, 8))
    fix = pltpu.make_async_remote_copy(
        fin.at[0], fin.at[1], fix_send, fix_recv, device_id=nxt, device_id_type=MESH
    )
    fix.start()

    def norm_body(n, carry):
        gain_sum, bias_sum = carry
        at = pl.ds(pl.multiple_of(n * 16, 16), 16)
        centred = (xj[at, :].astype(F32) - mean) * inverse
        normed = centred * gain + bias
        s = sigmoid(normed)
        grad = acc[at, :] * s * (1.0 + normed * (1.0 - s)) * valid_of(div(n, 4))
        weighted = grad * centred
        return (gain_sum + weighted[0:8] + weighted[8:16], bias_sum + grad[0:8] + grad[8:16])

    gain_sum, bias_sum = lax.fori_loop(0, CELLS_WIDE // 16, norm_body, (zero, zero))
    small_a[fr, 0:1] = jnp.sum(gain_sum, axis=0, keepdims=True)
    small_a[fr, 1:2] = jnp.sum(bias_sum, axis=0, keepdims=True)
    small_a[fr, 2:3] = jnp.sum(loss, axis=0, keepdims=True)
    small_a[fr, 3:8] = jnp.zeros((5, C), F32)
    for s in range(1, 8):
        copy = pltpu.make_async_remote_copy(
            small_a.at[fr], small_a.at[fr], a_send.at[s], a_recv.at[s],
            device_id=(dp, rem(fr + s, 8)), device_id_type=MESH,
        )
        copy.start()
        sends.append(copy)
    for s in range(1, 8):
        sender = rem(fr - s + 8, 8)
        pltpu.make_async_remote_copy(
            small_a.at[sender], small_a.at[sender], a_send.at[s], a_recv.at[s],
            device_id=(dp, sender), device_id_type=MESH,
        ).wait_recv()
    total = small_a[0]
    for f in range(1, 8):
        total = total + small_a[f]
    small_b[dp] = total
    for s in range(1, 16):
        copy = pltpu.make_async_remote_copy(
            small_b.at[dp], small_b.at[dp], b_send.at[s], b_recv.at[s],
            device_id=(rem(dp + s, 16), fr), device_id_type=MESH,
        )
        copy.start()
        sends.append(copy)
    for s in range(1, 16):
        sender = rem(dp - s + 16, 16)
        pltpu.make_async_remote_copy(
            small_b.at[sender], small_b.at[sender], b_send.at[s], b_recv.at[s],
            device_id=(sender, fr), device_id_type=MESH,
        ).wait_recv()
    total = small_b[0]
    for d in range(1, 16):
        total = total + small_b[d]
    small_out[...] = total

    fix.wait()
    rows_out[...] = fin[...]

    for copy in sends:
        copy.wait_send()
    pair_copy(hid_p, hid_p, 0).wait_send()
    pair_copy(go.at[0], go.at[1], 1).wait_send()
    pair_copy(s3_p, s3_p, 2).wait_send()
    pair_copy(gs.at[0], gs.at[1], 3).wait_send()
    for u in range(4):
        wait_sent(u, r1, r1_send, r1_recv)
        wait_sent(u, r2, r2_send, r2_recv)
        wait_sent(u, r3, r3_send, r3_recv)


def shards(clips_in, teacher, spatial_weight, temporal_weight, norm_gain, norm_bias):
    video = clips_in.reshape(ROWS, COLS, C)
    padded = jnp.pad(video, ((0, 0), (1, 1), (0, 0)))
    parts = jnp.stack([padded[:, OWN * d : OWN * d + WIDE] for d in range(FRAMES)])
    parts = parts.transpose(0, 2, 1, 3).reshape(FRAMES, WIDE * ROWS, C)
    target = teacher.reshape(ROWS, FRAMES, OWN, C).transpose(1, 2, 0, 3)
    target = target.reshape(FRAMES, OWN * ROWS, C)
    vmem = pl.BlockSpec(memory_space=pltpu.VMEM)
    hbm = pl.BlockSpec(memory_space=pl.ANY)
    dma = pltpu.SemaphoreType.DMA
    rows, small = pl.pallas_call(
        kernel,
        out_shape=(
            jax.ShapeDtypeStruct((2, 64, C), F32),
            jax.ShapeDtypeStruct((8, C), F32),
        ),
        in_specs=[vmem, hbm, vmem, vmem, hbm, hbm],
        out_specs=(vmem, vmem),
        scratch_shapes=[
            pltpu.VMEM((3, 3 * C, C), BF16),
            pltpu.VMEM((3 * C, C), BF16),
            pltpu.VMEM((FRAMES, WIDE * ROWS, C), BF16),
            pltpu.VMEM((FRAMES, OWN * ROWS, C), BF16),
            pltpu.VMEM((FRAMES, 16, C), F32),
            pltpu.VMEM((CELLS_WIDE, 3 * C), BF16),
            pltpu.VMEM((9 * C + 48, CELLS), BF16),
            pltpu.VMEM((8, 384, CELLS), BF16),
            pltpu.VMEM((CELLS, 3 * C), BF16),
            pltpu.VMEM((3 * C + 16, CELLS), BF16),
            pltpu.VMEM((8, 128, CELLS), BF16),
            pltpu.VMEM((CELLS, 3 * C), BF16),
            pltpu.VMEM((2, CELLS, C), BF16),
            pltpu.VMEM((2, CELLS, C), BF16),
            pltpu.VMEM((CELLS_WIDE, C), BF16),
            pltpu.VMEM((CELLS_WIDE, C), F32),
            pltpu.VMEM((4, 8, 8, BLOCK, C), BF16),
            pltpu.VMEM((4, 3, 16, BLOCK, C), BF16),
            pltpu.VMEM((4, 16, BLOCK, C), BF16),
            pltpu.VMEM((4, 3, 4, BLOCK, C), BF16),
            pltpu.VMEM((4, 4, BLOCK, C), F32),
            pltpu.VMEM((4, 3, BLOCK, C), F32),
            pltpu.VMEM((2, 64, C), F32),
            pltpu.VMEM((8, 8, C), F32),
            pltpu.VMEM((16, 8, C), F32),
            dma((10,)),
            dma((2,)),
            dma((8,)), dma((8,)),
            dma((8,)), dma((8,)),
            dma((8,)), dma((8,)),
            dma((4,)), dma((4,)),
            dma((4, 3)), dma((4, 3)),
            dma((4, 3)), dma((4, 3)),
            dma((4, 3)), dma((4, 3)),
            dma, dma,
            dma((8,)), dma((8,)),
            dma((16,)), dma((16,)),
        ],
        compiler_params=pltpu.CompilerParams(
            collective_id=0, has_side_effects=True, vmem_limit_bytes=64 * 2**20 - 2**17
        ),
    )(
        parts, target, norm_gain.reshape(1, C), norm_bias.reshape(1, C),
        spatial_weight, temporal_weight.reshape(3 * C, C),
    )
    chunk = rem(lax.axis_index("dp"), 2) * 8 + lax.axis_index("frame")
    both = jnp.concatenate([rows[1, 0:48], rows[0, 0:48]], axis=0)
    spatial_grad = lax.dynamic_slice(both, (48 - 3 * chunk, 0), (45, C))
    both = jnp.concatenate([rows[1, 48:64], rows[0, 48:64]], axis=0)
    temporal_grad = lax.dynamic_slice(both, (16 - chunk, 0), (15, C))
    loss = jnp.sum(small[2]) / float(16 * FRAMES * ROWS * COLS * C)
    return (spatial_grad, temporal_grad, small[0], small[1], loss)


def solution(mesh):
    return jax.shard_map(
        shards,
        mesh=mesh,
        in_specs=(
            P("dp", "frame", None, None, None),
            P("dp", "frame", None, None, None),
            P(),
            P(),
            P(),
            P(),
        ),
        out_specs=(P(("dp", "frame"), None), P(("dp", "frame"), None), P(), P(), P()),
        check_vma=False,
    )
```

```python
import jax
import jax.numpy as jnp
from jax import lax
from jax.experimental import pallas as pl
from jax.experimental.pallas import tpu as pltpu
from jax.sharding import PartitionSpec as P

GROUPS = 32
EPSILON = 1e-05
F32 = jnp.float32
BF16 = jnp.bfloat16
MESH = pl.DeviceIdType.MESH

FRAMES = 8
ROWS = 8
COLS = 96
C = 640
OWN = COLS // FRAMES
WIDE = OWN + 2
CELLS = OWN * FRAMES * ROWS
CELLS_WIDE = WIDE * FRAMES * ROWS
SLAB = FRAMES * ROWS
BLOCK = 16
TILES = C // 128
AXES = ((2, 0, 1), (1, 2, 0), (0, 1, 2), (0, 1, 2), (1, 2, 0), (2, 0, 1))
LANES = ((0, C), (0, C), (0, C), (0, 256), (256, 512), (512, C))
UNITS = 6


def rem(a, b):
    return lax.rem(a, jnp.int32(b))


def div(a, b):
    return lax.div(a, jnp.int32(b))


class Place:
    def __init__(self):
        self.dp = lax.axis_index("dp")
        self.fr = lax.axis_index("frame")
        self.core = rem(self.dp, 2)
        self.y = rem(div(self.dp, 2), 4)
        self.xh = div(self.dp, 8)
        self.z = div(self.fr, 2)
        self.xl = rem(self.fr, 2)
        self.x = 2 * self.xh + self.xl
        self.group = self.xh * 4 + self.y
        self.along = (self.x, self.y, self.z)

    def device(self, x, y, z):
        return (div(x, 2) * 8 + y * 2 + self.core, z * 2 + rem(x, 2))

    def moved(self, axis, there):
        at = [self.x, self.y, self.z]
        at[axis] = there
        return self.device(*at)

    def moved_two(self, first, one, second, two):
        at = [self.x, self.y, self.z]
        at[first] = one
        at[second] = two
        return self.device(*at)


def kernel(
    x_hbm, t_hbm, gain_ref, bias_ref, w_hbm, wt_hbm,
    rows_out, small_out,
    w, wt, xraw, traw, xs, ts, xr, tr, stats, hid, hid_t, hid_p, s3, s3_t, s3_p, go, gs, xj, acc,
    stage0, stage1, stage2, stage3, stage4, stage5,
    r10, r11, r12, r13, r14, r15,
    p20, p21, p22, p23, p24, p25,
    r20, r21, r22, r23, r24, r25,
    small_a, small_b,
    w_sem, own_sem, x_send, x_recv, t_send, t_recv, st_send, st_recv, pair_send, pair_recv,
    hp_send, hp_recv, r1_send, r1_recv, r2_send, r2_recv, a_send, a_recv, b_send, b_recv,
):
    me = Place()
    dp, fr, core = me.dp, me.fr, me.core
    gs3 = s3
    g3 = hid
    stage = (stage0, stage1, stage2, stage3, stage4, stage5)
    r1 = (r10, r11, r12, r13, r14, r15)
    p2 = (p20, p21, p22, p23, p24, p25)
    r2 = (r20, r21, r22, r23, r24, r25)

    def get(at):
        return jnp.concatenate([acc[l, at, :] for l in range(TILES)], axis=1)

    def put(at, value):
        for l in range(TILES):
            acc[l, at, :] = value[:, l * 128 : (l + 1) * 128]

    load_x = pltpu.make_async_copy(x_hbm, xraw, own_sem.at[0])
    load_x.start()
    load_t = pltpu.make_async_copy(t_hbm, traw, own_sem.at[1])
    load_t.start()

    w_copies = []
    for a in range(3):
        for c in range(3):
            w_copies.append(
                pltpu.make_async_copy(
                    w_hbm.at[a, c], w.at[c, pl.ds(a * C, C)], w_sem.at[3 * a + c]
                )
            )
    w_copies.append(pltpu.make_async_copy(wt_hbm, wt, w_sem.at[9]))
    for copy in w_copies:
        copy.start()

    barrier = pltpu.get_barrier_semaphore()

    def greet(device):
        pl.semaphore_signal(barrier, inc=1, device_id=device, device_id_type=MESH)

    for axis in range(3):
        for s in range(1, 4):
            greet(me.moved(axis, rem(me.along[axis] + s, 4)))
    for one, two in ((0, 1), (1, 2), (0, 2)):
        for s in range(1, 4):
            for t in range(1, 4):
                greet(
                    me.moved_two(
                        one, rem(me.along[one] + s, 4), two, rem(me.along[two] + t, 4)
                    )
                )
    across = 1 - 2 * core
    for s in range(4):
        greet((me.xh * 8 + rem(me.y + s, 4) * 2 + core + across, fr))
    partner = (dp + across, fr)

    load_x.wait()

    def moment_body(i, carry):
        total, square = carry
        v = xraw[i].astype(F32)
        put(pl.ds(pl.multiple_of(i * COLS, 8), COLS), v)
        v = v.reshape(COLS // 8, 8, C)
        return (total + jnp.sum(v, axis=0), square + jnp.sum(v * v, axis=0))

    zero = jnp.zeros((8, C), F32)
    total, square = lax.fori_loop(0, ROWS, moment_body, (zero, zero))
    stats[fr, 0:8] = total
    stats[fr, 8:16] = square

    pl.semaphore_wait(barrier, 40)

    sends = []
    for s in range(1, 8):
        to = rem(fr + s, 8)
        copy = pltpu.make_async_remote_copy(
            stats.at[fr], stats.at[fr], st_send.at[s], st_recv.at[s],
            device_id=(dp, to), device_id_type=MESH,
        )
        copy.start()
        sends.append(copy)

    def two_columns(first, second):
        return jnp.concatenate(
            [
                jnp.concatenate(
                    [acc[l, pl.ds(j, ROWS, stride=COLS), :] for l in range(TILES)], axis=1
                )
                for j in (first, second)
            ],
            axis=0,
        ).astype(BF16)

    def x_share(ref, to):
        def body(jj, carry):
            j = OWN * to - 1 + 2 * jj
            ref[pl.ds(pl.multiple_of(16 * jj, 16), 16), :] = two_columns(
                jnp.maximum(j, 0), jnp.minimum(j + 1, COLS - 1)
            )
            return carry

        lax.fori_loop(0, WIDE // 2, body, 0)

    def t_share(ref, to):
        def body(jj, carry):
            j = OWN * to + 2 * jj
            ref[pl.ds(pl.multiple_of(16 * jj, 16), 16), :] = two_columns(j, j + 1)
            return carry

        lax.fori_loop(0, OWN // 2, body, 0)

    for s in range(1, 8):
        to = rem(fr + s, 8)
        x_share(xs.at[s], to)
        copy = pltpu.make_async_remote_copy(
            xs.at[s], xr.at[fr], x_send.at[s], x_recv.at[s],
            device_id=(dp, to), device_id_type=MESH,
        )
        copy.start()
        sends.append(copy)
    x_share(xr.at[fr], fr)

    load_t.wait()

    def teacher_body(i, carry):
        put(pl.ds(pl.multiple_of(i * COLS, 8), COLS), traw[i].astype(F32))
        return carry

    lax.fori_loop(0, ROWS, teacher_body, 0)
    for s in range(1, 8):
        to = rem(fr + s, 8)
        t_share(ts.at[s], to)
        copy = pltpu.make_async_remote_copy(
            ts.at[s], tr.at[fr], t_send.at[s], t_recv.at[s],
            device_id=(dp, to), device_id_type=MESH,
        )
        copy.start()
        sends.append(copy)
    t_share(tr.at[fr], fr)

    hid_t[9 * C :, :] = jnp.zeros((48, CELLS), BF16)
    s3_t[3 * C :, :] = jnp.zeros((16, CELLS), BF16)

    row = lax.broadcasted_iota(jnp.int32, (C, C), 0)
    col = lax.broadcasted_iota(jnp.int32, (C, C), 1)
    same = (
        lax.shift_right_logical(row * 3277, 16) == lax.shift_right_logical(col * 3277, 16)
    ).astype(F32)
    for s in range(1, 8):
        sender = rem(fr - s + 8, 8)
        pltpu.make_async_remote_copy(
            stats.at[sender], stats.at[sender], st_send.at[s], st_recv.at[s],
            device_id=(dp, sender), device_id_type=MESH,
        ).wait_recv()
    moments = stats[0]
    for f in range(1, FRAMES):
        moments = moments + stats[f]
    wide = jnp.dot(moments, same, precision=lax.Precision.HIGHEST, preferred_element_type=F32)
    size = float(FRAMES * ROWS * COLS * (C // GROUPS))
    mean = jnp.sum(wide[0:8], axis=0, keepdims=True) / size
    variance = jnp.sum(wide[8:16], axis=0, keepdims=True) / size - mean * mean
    inverse = lax.rsqrt(variance + EPSILON)
    gain = gain_ref[...].reshape(1, C)
    bias = bias_ref[...].reshape(1, C)

    for s in range(1, 8):
        sender = rem(fr - s + 8, 8)
        pltpu.make_async_remote_copy(
            xr.at[sender], xr.at[sender], x_send.at[s], x_recv.at[s],
            device_id=(dp, sender), device_id_type=MESH,
        ).wait_recv()

    cell_row = rem(lax.broadcasted_iota(jnp.int32, (BLOCK, C), 0), 8)

    def valid_of(j):
        outside = ((j == 0) & (fr == 0)) | ((j == WIDE - 1) & (fr == FRAMES - 1))
        return 1.0 - outside.astype(F32)

    def sigmoid(v):
        return 0.5 * jnp.tanh(0.5 * v) + 0.5

    def store_row_shifts(ref, at, value, first, last):
        ref[at, first * C : (first + 1) * C] = jnp.where(
            cell_row == 0, 0.0, pltpu.roll(value, 1, 0)
        ).astype(BF16)
        ref[at, C : 2 * C] = value.astype(BF16)
        ref[at, last * C : (last + 1) * C] = jnp.where(
            cell_row == 7, 0.0, pltpu.roll(value, BLOCK - 1, 0)
        ).astype(BF16)

    def hidden_body(n, carry):
        p = div(n, WIDE // 2)
        jj = rem(n, WIDE // 2)
        at = pl.ds(pl.multiple_of(jj * 16, 16), 16)
        even = xr[2 * p, at].astype(F32)
        odd = xr[2 * p + 1, at].astype(F32)
        for h in range(2):
            j = 2 * jj + h
            v = jnp.concatenate([even[8 * h : 8 * h + 8], odd[8 * h : 8 * h + 8]], axis=0)
            normed = (v - mean) * inverse * gain + bias
            value = normed * sigmoid(normed) * valid_of(j)
            dst = pl.ds(pl.multiple_of(j * SLAB + p * 16, 16), 16)
            xj[dst, :] = v.astype(BF16)
            store_row_shifts(hid, dst, value, 0, 2)
        return carry

    lax.fori_loop(0, 4 * (WIDE // 2), hidden_body, 0)

    def pair_copy(src, dst, n):
        return pltpu.make_async_remote_copy(
            src, dst, pair_send.at[n], pair_recv.at[n], device_id=partner, device_id_type=MESH
        )

    for copy in w_copies:
        copy.wait()

    def conv_body(b, carry):
        total = None
        for c in range(3):
            src = pl.ds(pl.multiple_of(b * 256 + c * SLAB, 64), 256)
            part = jnp.dot(hid[src, :], w[c], preferred_element_type=F32)
            total = part if total is None else total + part
            for a in range(3):
                top = (a * 3 + c) * C
                for half in range(2):
                    src = pl.ds(pl.multiple_of(b * 256 + c * SLAB + half * 128, 64), 128)
                    dst = pl.ds(pl.multiple_of(b * 256 + half * 128, 128), 128)
                    hid_t[top : top + C, dst] = hid[src, a * C : (a + 1) * C].T
        put(pl.ds(pl.multiple_of(b * 256, 256), 256), total)
        return carry

    lax.fori_loop(0, 3, conv_body, 0)

    def hidden_pair(m):
        src = pl.ds(pl.multiple_of(720 * m + 352 * (1 - core), 16), 384)
        return pltpu.make_async_remote_copy(
            hid_t.at[src], hid_p.at[m], hp_send.at[m], hp_recv.at[m],
            device_id=partner, device_id_type=MESH,
        )

    def hidden_send(n, carry):
        hidden_pair(rem(me.group + 1 + n, 8)).start()
        return carry

    lax.fori_loop(0, 8, hidden_send, 0)

    pad8 = jnp.zeros((8, C), F32)

    def store_frame_shifts(ref, at, value, before, after):
        ref[at, before * C : (before + 1) * C] = jnp.concatenate(
            [pad8, value[: SLAB - 8]], axis=0
        ).astype(BF16)
        ref[at, C : 2 * C] = value.astype(BF16)
        ref[at, after * C : (after + 1) * C] = jnp.concatenate(
            [value[8:], pad8], axis=0
        ).astype(BF16)

    def state_body(j, carry):
        at = pl.ds(pl.multiple_of(j * SLAB, SLAB), SLAB)
        store_frame_shifts(s3, at, get(at), 0, 2)
        return carry

    lax.fori_loop(0, OWN, state_body, 0)

    def temporal_body(b, carry):
        src = pl.ds(pl.multiple_of(b * 256, 256), 256)
        put(src, jnp.dot(s3[src, :], wt[...], preferred_element_type=F32))
        for t in range(3):
            for half in range(2):
                at = pl.ds(pl.multiple_of(b * 256 + half * 128, 128), 128)
                s3_t[t * C : (t + 1) * C, at] = s3[at, t * C : (t + 1) * C].T
        return carry

    lax.fori_loop(0, 3, temporal_body, 0)
    for m in range(8):
        src = pl.ds(pl.multiple_of(240 * m + 112 * (1 - core), 16), 144)
        pair_copy(s3_t.at[src], s3_p.at[m], 2).start()

    for s in range(1, 8):
        sender = rem(fr - s + 8, 8)
        pltpu.make_async_remote_copy(
            tr.at[sender], tr.at[sender], t_send.at[s], t_recv.at[s],
            device_id=(dp, sender), device_id_type=MESH,
        ).wait_recv()

    scale = float(16 * FRAMES * ROWS * COLS) ** (-0.5)

    def error_body(jj, loss):
        at = pl.ds(pl.multiple_of(jj * 16, 16), 16)
        target = [tr[f, at].astype(F32) for f in range(FRAMES)]
        for h in range(2):
            j = 2 * jj + h
            own = pl.ds(pl.multiple_of(j * SLAB, SLAB), SLAB)
            wide_at = pl.ds(pl.multiple_of((j + 1) * SLAB, SLAB), SLAB)
            taught = jnp.concatenate([t[8 * h : 8 * h + 8] for t in target], axis=0)
            out = get(own).astype(BF16).astype(F32)
            error = xj[wide_at, :].astype(F32) + out - taught
            grad = error * scale
            go[0, own, :] = grad.astype(BF16)
            store_frame_shifts(g3, own, grad, 2, 0)
            loss = loss + jnp.sum((error * error).reshape(FRAMES, 8, C), axis=0)
        return loss

    loss = lax.fori_loop(0, OWN // 2, error_body, jnp.zeros((8, C), F32))
    pair_copy(go.at[0], go.at[1], 1).start()

    def nt(lhs, rhs):
        return lax.dot_general(lhs, rhs, (((1,), (1,)), ((), ())), preferred_element_type=F32)

    def state_grad_body(b, carry):
        src = pl.ds(pl.multiple_of(b * 256, 256), 256)
        total = None
        for t in range(3):
            part = nt(g3[src, t * C : (t + 1) * C], wt[t * C : (t + 1) * C, :])
            total = part if total is None else total + part
        put(src, total)
        return carry

    lax.fori_loop(0, 3, state_grad_body, 0)

    def grad_state_body(b, carry):
        at = pl.ds(pl.multiple_of(b * 16, 16), 16)
        value = get(at)
        gs[0, at, :] = value.astype(BF16)
        store_row_shifts(gs3, at, value, 2, 0)
        return carry

    lax.fori_loop(0, CELLS // 16, grad_state_body, 0)
    pair_copy(gs.at[0], gs.at[1], 3).start()

    def wait_pair(dst, n):
        pair_copy(dst, dst, n).wait_recv()

    wait_pair(go.at[1], 1)
    wait_pair(s3_p, 2)

    def time_body(n, carry):
        own = jnp.concatenate(
            [
                s3_t[pl.ds(pl.multiple_of(240 * (4 * n + k) + 112 * core, 16), 144), :]
                for k in range(4)
            ],
            axis=0,
        )
        other = s3_p[pl.ds(4 * n, 4)].reshape(576, CELLS)
        out = jnp.dot(own, go[0], preferred_element_type=F32)
        put(pl.ds(0, 576), out + jnp.dot(other, go[1], preferred_element_type=F32))
        for k in range(4):
            for q in range(8):
                cut = 15 * q % 8
                at = pl.ds(pl.multiple_of(144 * k + 15 * q - cut + 8 * core, 8), 24)
                rows = get(at)[cut : cut + 16].astype(BF16)
                zz, xl = q // 2, q % 2
                stage[3][4 * n + k, xl * 4 + zz] = rows[:, 0:256]
                stage[4][4 * n + k, q] = rows[:, 256:512]
                stage[5][4 * n + k, q] = rows[:, 512:C]
        return carry

    lax.fori_loop(0, 2, time_body, 0)

    def first_send(u, src, step, dst, device):
        pltpu.make_async_remote_copy(
            src, dst, r1_send.at[u, step - 1], r1_recv.at[u, step - 1],
            device_id=device, device_id_type=MESH,
        ).start()

    def send_y(u, m):
        mx, my = div(m, 4), rem(m, 4)
        step = rem(my - me.y + 4, 4)

        @pl.when(step != 0)
        def _():
            first_send(
                u, stage[u].at[m], step,
                r1[u].at[step - 1, pl.ds(mx * 8, 8)], me.moved(1, my),
            )

    def send_z(u, m):
        for s in range(1, 4):
            there = rem(me.z + s, 4)
            first_send(
                u, stage[u].at[m, pl.ds(there * 2, 2)], s,
                r1[u].at[s - 1, pl.ds(m * 2, 2)], me.moved(2, there),
            )

    def send_x(u, m):
        mx, my = div(m, 4), rem(m, 4)
        for xl in range(2):
            there = 2 * mx + xl
            step = rem(there - me.x + 4, 4)

            @pl.when(step != 0)
            def _():
                first_send(
                    u, stage[u].at[m, pl.ds(xl * 4, 4)], step,
                    r1[u].at[step - 1, pl.ds(my * 4, 4)], me.moved(0, there),
                )

    def time_send(n, carry):
        m = rem(me.group + 1 + n, 8)
        send_x(3, m)
        send_y(4, m)
        send_z(5, m)
        return carry

    lax.fori_loop(0, 8, time_send, 0)

    wait_pair(gs.at[1], 3)

    def space_body(n, carry):
        m = rem(me.group + 1 + n, 8)
        hidden_pair(m).wait_recv()
        own = hid_t[pl.ds(pl.multiple_of(720 * m + 352 * core, 16), 384), :]
        out = jnp.dot(own, gs[0], preferred_element_type=F32)
        put(pl.ds(0, 384), out + jnp.dot(hid_p[m], gs[1], preferred_element_type=F32))
        for q in range(8):
            cut = 45 * q % 8
            at = pl.ds(pl.multiple_of(45 * q - cut + 8 * core, 8), 56)
            rows = get(at)[cut : cut + 48].astype(BF16)
            zz, xl = q // 2, q % 2
            stage[0][m, q] = rows[0:16]
            stage[1][m, q] = rows[16:32]
            stage[2][m, xl * 4 + zz] = rows[32:48]
        send_z(0, m)
        send_y(1, m)
        send_x(2, m)
        return carry

    lax.fori_loop(0, 8, space_body, 0)

    def clear_body(b, carry):
        put(pl.ds(pl.multiple_of(b * SLAB, SLAB), SLAB), jnp.zeros((SLAB, C), F32))
        return carry

    lax.fori_loop(0, WIDE, clear_body, 0)

    def grad_hidden(c):
        def body(b, carry):
            src = pl.ds(pl.multiple_of(b * 256, 256), 256)
            dst = pl.ds(pl.multiple_of(b * 256 + c * SLAB, 64), 256)
            total = get(dst)
            for a in range(3):
                total = total + nt(gs3[src, a * C : (a + 1) * C], w[c, a * C : (a + 1) * C, :])
            put(dst, total)
            return carry

        lax.fori_loop(0, 3, body, 0)

    def first_steps(u, wait):
        for s in range(1, 4):
            copy = pltpu.make_async_remote_copy(
                r1[u].at[s - 1], r1[u].at[s - 1], r1_send.at[u, s - 1], r1_recv.at[u, s - 1],
                device_id=me.moved(0, rem(me.x + 1, 4)), device_id_type=MESH,
            )
            if wait == "recv":
                copy.wait_recv()
            else:
                copy.wait_send()

    def plane_copy(u, src, dst, device):
        return pltpu.make_async_remote_copy(
            src, dst, r2_send.at[u], r2_recv.at[u], device_id=device, device_id_type=MESH
        )

    def plane_all(u):
        return plane_copy(u, r2[u], r2[u], me.moved(0, rem(me.x + 1, 4)))

    def second_phase(u):
        first_steps(u, "recv")
        axis, one, two = AXES[u]

        def body(k, carry):
            if axis == 2:
                m, xl = div(k, 2), rem(k, 2)
                own = stage[u][m, 2 * me.z + xl]
                to = (2 * div(m, 4) + xl) * 4 + rem(m, 4)
            elif axis == 0:
                own = stage[u][me.xh * 4 + div(k, 4), me.xl * 4 + rem(k, 4)]
                to = k
            else:
                mx, q = div(k, 8), rem(k, 8)
                own = stage[u][mx * 4 + me.y, q]
                to = div(q, 2) * 4 + mx * 2 + rem(q, 2)
            total = own.astype(F32)
            for s in range(3):
                total = total + r1[u][s, k].astype(F32)
            p2[u][to] = total.astype(BF16)
            return carry

        lax.fori_loop(0, 16, body, 0)

        def send(n, carry):
            there_one = rem(me.along[one] + div(n, 4), 4)
            there_two = rem(me.along[two] + rem(n, 4), 4)
            plane_copy(
                u, p2[u].at[there_one * 4 + there_two], r2[u].at[n - 1],
                me.moved_two(one, there_one, two, there_two),
            ).start()
            return carry

        lax.fori_loop(1, 16, send, 0)

    def last_phase(u):
        plane_all(u).wait_recv()
        axis, one, two = AXES[u]
        total = p2[u][me.along[one] * 4 + me.along[two]].astype(F32)
        for n in range(15):
            total = total + r2[u][n].astype(F32)
        low, high = LANES[u]
        top = min(u, 3) * BLOCK
        rows_out[top : top + BLOCK, low:high] = total

    grad_hidden(0)
    for u in range(3, 6):
        second_phase(u)
    grad_hidden(1)
    grad_hidden(2)

    def norm_body(n, carry):
        gain_sum, bias_sum = carry
        at = pl.ds(pl.multiple_of(n * 16, 16), 16)
        centred = (xj[at, :].astype(F32) - mean) * inverse
        normed = centred * gain + bias
        s = sigmoid(normed)
        grad = get(at) * s * (1.0 + normed * (1.0 - s)) * valid_of(div(n, 4))
        weighted = grad * centred
        return (gain_sum + weighted[0:8] + weighted[8:16], bias_sum + grad[0:8] + grad[8:16])

    gain_sum, bias_sum = lax.fori_loop(0, CELLS_WIDE // 16, norm_body, (zero, zero))
    at_plane = me.x * 4 + me.z
    small_a[at_plane, 0:1] = jnp.sum(gain_sum, axis=0, keepdims=True)
    small_a[at_plane, 1:2] = jnp.sum(bias_sum, axis=0, keepdims=True)
    small_a[at_plane, 2:3] = jnp.sum(loss, axis=0, keepdims=True)
    small_a[at_plane, 3:8] = jnp.zeros((5, C), F32)

    def small_one(n, carry):
        to = me.moved_two(0, rem(me.x + div(n, 4), 4), 2, rem(me.z + rem(n, 4), 4))
        pltpu.make_async_remote_copy(
            small_a.at[at_plane], small_a.at[at_plane], a_send, a_recv,
            device_id=to, device_id_type=MESH,
        ).start()
        return carry

    lax.fori_loop(1, 16, small_one, 0)

    for u in range(3):
        second_phase(u)

    small_all = pltpu.make_async_remote_copy(
        small_a.at[pl.ds(0, 15)], small_a.at[pl.ds(0, 15)], a_send, a_recv,
        device_id=partner, device_id_type=MESH,
    )
    small_all.wait_recv()
    total = small_a[0]
    for f in range(1, 16):
        total = total + small_a[f]
    at_rest = me.y * 2 + core
    small_b[at_rest] = total
    for s in range(4):
        for t in range(2):
            if s + t > 0:
                other = core + t * across
                to = (me.xh * 8 + rem(me.y + s, 4) * 2 + other, fr)
                pltpu.make_async_remote_copy(
                    small_b.at[at_rest], small_b.at[at_rest], b_send, b_recv,
                    device_id=to, device_id_type=MESH,
                ).start()

    for u in range(3, 6):
        last_phase(u)

    rest_all = pltpu.make_async_remote_copy(
        small_b.at[pl.ds(0, 7)], small_b.at[pl.ds(0, 7)], b_send, b_recv,
        device_id=partner, device_id_type=MESH,
    )
    rest_all.wait_recv()
    total = small_b[0]
    for d in range(1, 8):
        total = total + small_b[d]
    small_out[...] = total

    for u in range(3):
        last_phase(u)

    for copy in sends:
        copy.wait_send()
    small_all.wait_send()
    rest_all.wait_send()
    for m in range(8):
        hidden_pair(m).wait_send()
    pair_copy(go.at[0], go.at[1], 1).wait_send()
    pair_copy(s3_p, s3_p, 2).wait_send()
    pair_copy(gs.at[0], gs.at[1], 3).wait_send()
    for u in range(UNITS):
        first_steps(u, "send")
        plane_all(u).wait_send()


def finish(rows, small, space, time, gain, bias, loss):
    space[...] = rows[0:45]
    time[...] = rows[48:63]
    gain[...] = small[0]
    bias[...] = small[1]
    loss[0, 0] = jnp.sum(small[2:3]) / float(16 * FRAMES * ROWS * COLS * C)


def shards(clips_in, teacher, spatial_weight, temporal_weight, norm_gain, norm_bias):
    vmem = pl.BlockSpec(memory_space=pltpu.VMEM)
    hbm = pl.BlockSpec(memory_space=pl.ANY)
    dma = pltpu.SemaphoreType.DMA
    wide = [high - low for low, high in LANES]
    rows, small = pl.pallas_call(
        kernel,
        out_shape=(
            jax.ShapeDtypeStruct((64, C), F32),
            jax.ShapeDtypeStruct((8, C), F32),
        ),
        in_specs=[hbm, hbm, vmem, vmem, hbm, hbm],
        out_specs=(vmem, vmem),
        scratch_shapes=[
            pltpu.VMEM((3, 3 * C, C), BF16),
            pltpu.VMEM((3 * C, C), BF16),
            pltpu.VMEM((ROWS, COLS, C), BF16),
            pltpu.VMEM((ROWS, COLS, C), BF16),
            pltpu.VMEM((FRAMES, WIDE * ROWS, C), BF16),
            pltpu.VMEM((FRAMES, OWN * ROWS, C), BF16),
            pltpu.VMEM((FRAMES, WIDE * ROWS, C), BF16),
            pltpu.VMEM((FRAMES, OWN * ROWS, C), BF16),
            pltpu.VMEM((FRAMES, 16, C), F32),
            pltpu.VMEM((CELLS_WIDE, 3 * C), BF16),
            pltpu.VMEM((9 * C + 48, CELLS), BF16),
            pltpu.VMEM((8, 384, CELLS), BF16),
            pltpu.VMEM((CELLS, 3 * C), BF16),
            pltpu.VMEM((3 * C + 16, CELLS), BF16),
            pltpu.VMEM((8, 144, CELLS), BF16),
            pltpu.VMEM((2, CELLS, C), BF16),
            pltpu.VMEM((2, CELLS, C), BF16),
            pltpu.VMEM((CELLS_WIDE, C), BF16),
            pltpu.VMEM((TILES, CELLS_WIDE, 128), F32),
            *[pltpu.VMEM((8, 8, BLOCK, n), BF16) for n in wide],
            *[pltpu.VMEM((3, 16, BLOCK, n), BF16) for n in wide],
            *[pltpu.VMEM((16, BLOCK, n), BF16) for n in wide],
            *[pltpu.VMEM((15, BLOCK, n), BF16) for n in wide],
            pltpu.VMEM((16, 8, C), F32),
            pltpu.VMEM((8, 8, C), F32),
            dma((10,)),
            dma((2,)),
            dma((8,)), dma((8,)),
            dma((8,)), dma((8,)),
            dma((8,)), dma((8,)),
            dma((4,)), dma((4,)),
            dma((8,)), dma((8,)),
            dma((UNITS, 3)), dma((UNITS, 3)),
            dma((UNITS,)), dma((UNITS,)),
            dma, dma,
            dma, dma,
        ],
        compiler_params=pltpu.CompilerParams(
            collective_id=0, has_side_effects=True, vmem_limit_bytes=64 * 2**20 - 2**17
        ),
    )(
        clips_in.reshape(ROWS, COLS, C), teacher.reshape(ROWS, COLS, C), norm_gain, norm_bias,
        spatial_weight, temporal_weight.reshape(3 * C, C),
    )
    spatial_grad, temporal_grad, gain_grad, bias_grad, loss = pl.pallas_call(
        finish,
        out_shape=(
            jax.ShapeDtypeStruct((45, C), F32),
            jax.ShapeDtypeStruct((15, C), F32),
            jax.ShapeDtypeStruct((C,), F32),
            jax.ShapeDtypeStruct((C,), F32),
            jax.ShapeDtypeStruct((1, 1), F32),
        ),
        in_specs=[vmem, vmem],
        out_specs=(vmem, vmem, vmem, vmem, pl.BlockSpec(memory_space=pltpu.SMEM)),
    )(rows, small)
    return (spatial_grad, temporal_grad, gain_grad, bias_grad, loss.reshape(()))


def solution(mesh):
    return jax.shard_map(
        shards,
        mesh=mesh,
        in_specs=(
            P("dp", "frame", None, None, None),
            P("dp", "frame", None, None, None),
            P(),
            P(),
            P(),
            P(),
        ),
        out_specs=(P(("dp", "frame"), None), P(("dp", "frame"), None), P(), P(), P()),
        check_vma=False,
    )
```

```python
import jax
import jax.numpy as jnp
from jax import lax
from jax.experimental import pallas as pl
from jax.experimental.pallas import tpu as pltpu
from jax.sharding import PartitionSpec as P

GROUPS = 32
EPSILON = 1e-05
F32 = jnp.float32
BF16 = jnp.bfloat16
MESH = pl.DeviceIdType.MESH

FRAMES = 8
ROWS = 8
COLS = 96
C = 640
OWN = COLS // FRAMES
WIDE = OWN + 2
CELLS = OWN * FRAMES * ROWS
CELLS_WIDE = WIDE * FRAMES * ROWS
SLAB = FRAMES * ROWS
BLOCK = 16
TILES = C // 128
AXES = ((2, 0, 1), (1, 2, 0), (0, 1, 2), (0, 1, 2), (1, 2, 0), (2, 0, 1))
LANES = ((0, C), (0, C), (0, C), (0, 256), (256, 512), (512, C))
UNITS = 6


def rem(a, b):
    return lax.rem(a, jnp.int32(b))


def div(a, b):
    return lax.div(a, jnp.int32(b))


class Place:
    def __init__(self):
        self.dp = lax.axis_index("dp")
        self.fr = lax.axis_index("frame")
        self.core = rem(self.dp, 2)
        self.y = rem(div(self.dp, 2), 4)
        self.xh = div(self.dp, 8)
        self.z = div(self.fr, 2)
        self.xl = rem(self.fr, 2)
        self.x = 2 * self.xh + self.xl
        self.group = self.xh * 4 + self.y
        self.along = (self.x, self.y, self.z)

        self.at = [[rem(v + step, 4) for step in range(4)] for v in self.along]
        self.dp_x = [div(v, 2) * 8 for v in self.at[0]]
        self.fr_x = [rem(v, 2) for v in self.at[0]]
        self.dp_y = [2 * v for v in self.at[1]]
        self.fr_z = [2 * v for v in self.at[2]]

    def further(self, *steps):
        x, y, z = steps
        return (self.dp_x[x] + self.dp_y[y] + self.core, self.fr_z[z] + self.fr_x[x])

    def along_axis(self, axis, step):
        return self.further(*(step if axis == n else 0 for n in range(3)))

    def in_plane(self, one, step_one, two, step_two):
        return self.further(
            *(step_one if n == one else step_two if n == two else 0 for n in range(3))
        )


def kernel(
    x_hbm, t_hbm, gain_ref, bias_ref, w_hbm, wt_hbm,
    rows_out, small_out,
    w, wt, xraw, traw, xs, ts, xr, tr, stats, hid, hid_t, hid_p, s3, s3_t, s3_p, go, gs, xj, acc,
    stage0, stage1, stage2, stage3, stage4, stage5,
    r10, r11, r12, r13, r14, r15,
    p20, p21, p22, p23, p24, p25,
    r20, r21, r22, r23, r24, r25,
    small_a, small_b,
    w_sem, own_sem, x_send, x_recv, t_send, t_recv, st_send, st_recv, pair_send, pair_recv,
    hp_send, hp_recv, r1_send, r1_recv, r2_send, r2_recv, a_send, a_recv, b_send, b_recv,
):
    me = Place()
    dp, fr, core = me.dp, me.fr, me.core
    gs3 = s3
    g3 = hid
    stage = (stage0, stage1, stage2, stage3, stage4, stage5)
    r1 = (r10, r11, r12, r13, r14, r15)
    p2 = (p20, p21, p22, p23, p24, p25)
    r2 = (r20, r21, r22, r23, r24, r25)

    def get(at):
        return jnp.concatenate([acc[l, at, :] for l in range(TILES)], axis=1)

    def put(at, value):
        for l in range(TILES):
            acc[l, at, :] = value[:, l * 128 : (l + 1) * 128]

    load_x = pltpu.make_async_copy(x_hbm, xraw, own_sem.at[0])
    load_x.start()
    load_t = pltpu.make_async_copy(t_hbm, traw, own_sem.at[1])
    load_t.start()

    w_copies = []
    for a in range(3):
        for c in range(3):
            w_copies.append(
                pltpu.make_async_copy(
                    w_hbm.at[a, c], w.at[c, pl.ds(a * C, C)], w_sem.at[3 * a + c]
                )
            )
    w_copies.append(pltpu.make_async_copy(wt_hbm, wt, w_sem.at[9]))
    for copy in w_copies:
        copy.start()

    barrier = pltpu.get_barrier_semaphore()

    def greet(device):
        pl.semaphore_signal(barrier, inc=1, device_id=device, device_id_type=MESH)

    for axis in range(3):
        for s in range(1, 4):
            greet(me.along_axis(axis, s))
    for one, two in ((0, 1), (1, 2), (0, 2)):
        for s in range(1, 4):
            for t in range(1, 4):
                greet(me.in_plane(one, s, two, t))
    across = 1 - 2 * core
    for s in range(4):
        greet((me.dp_x[0] + me.dp_y[s] + core + across, fr))
    partner = (dp + across, fr)

    load_x.wait()

    def moment_body(i, carry):
        total, square = carry
        v = xraw[i].astype(F32)
        put(pl.ds(pl.multiple_of(i * COLS, 8), COLS), v)
        v = v.reshape(COLS // 8, 8, C)
        return (total + jnp.sum(v, axis=0), square + jnp.sum(v * v, axis=0))

    zero = jnp.zeros((8, C), F32)
    total, square = lax.fori_loop(0, ROWS, moment_body, (zero, zero))
    stats[fr, 0:8] = total
    stats[fr, 8:16] = square

    pl.semaphore_wait(barrier, 40)

    sends = []
    for s in range(1, 8):
        to = rem(fr + s, 8)
        copy = pltpu.make_async_remote_copy(
            stats.at[fr], stats.at[fr], st_send.at[s], st_recv.at[s],
            device_id=(dp, to), device_id_type=MESH,
        )
        copy.start()
        sends.append(copy)

    def two_columns(first, second):
        return jnp.concatenate(
            [
                jnp.concatenate(
                    [acc[l, pl.ds(j, ROWS, stride=COLS), :] for l in range(TILES)], axis=1
                )
                for j in (first, second)
            ],
            axis=0,
        ).astype(BF16)

    def x_share(ref, to):
        def body(jj, carry):
            j = OWN * to - 1 + 2 * jj
            ref[pl.ds(pl.multiple_of(16 * jj, 16), 16), :] = two_columns(
                jnp.maximum(j, 0), jnp.minimum(j + 1, COLS - 1)
            )
            return carry

        lax.fori_loop(0, WIDE // 2, body, 0)

    def t_share(ref, to):
        def body(jj, carry):
            j = OWN * to + 2 * jj
            ref[pl.ds(pl.multiple_of(16 * jj, 16), 16), :] = two_columns(j, j + 1)
            return carry

        lax.fori_loop(0, OWN // 2, body, 0)

    for s in range(1, 8):
        to = rem(fr + s, 8)
        x_share(xs.at[s], to)
        copy = pltpu.make_async_remote_copy(
            xs.at[s], xr.at[fr], x_send.at[s], x_recv.at[s],
            device_id=(dp, to), device_id_type=MESH,
        )
        copy.start()
        sends.append(copy)
    x_share(xr.at[fr], fr)

    load_t.wait()

    def teacher_body(i, carry):
        put(pl.ds(pl.multiple_of(i * COLS, 8), COLS), traw[i].astype(F32))
        return carry

    lax.fori_loop(0, ROWS, teacher_body, 0)
    for s in range(1, 8):
        to = rem(fr + s, 8)
        t_share(ts.at[s], to)
    t_share(tr.at[fr], fr)

    hid_t[9 * C :, :] = jnp.zeros((48, CELLS), BF16)
    s3_t[3 * C :, :] = jnp.zeros((16, CELLS), BF16)

    row = lax.broadcasted_iota(jnp.int32, (C, C), 0)
    col = lax.broadcasted_iota(jnp.int32, (C, C), 1)
    same = (
        lax.shift_right_logical(row * 3277, 16) == lax.shift_right_logical(col * 3277, 16)
    ).astype(F32).astype(BF16)
    for s in range(1, 8):
        sender = rem(fr - s + 8, 8)
        pltpu.make_async_remote_copy(
            stats.at[sender], stats.at[sender], st_send.at[s], st_recv.at[s],
            device_id=(dp, sender), device_id_type=MESH,
        ).wait_recv()
    moments = stats[0]
    for f in range(1, FRAMES):
        moments = moments + stats[f]
    high = moments.astype(BF16)
    rest = moments - high.astype(F32)
    middle = rest.astype(BF16)
    low = (rest - middle.astype(F32)).astype(BF16)
    wide = (
        jnp.dot(high, same, preferred_element_type=F32)
        + jnp.dot(middle, same, preferred_element_type=F32)
        + jnp.dot(low, same, preferred_element_type=F32)
    )
    size = float(FRAMES * ROWS * COLS * (C // GROUPS))
    mean = jnp.sum(wide[0:8], axis=0, keepdims=True) / size
    variance = jnp.sum(wide[8:16], axis=0, keepdims=True) / size - mean * mean
    inverse = lax.rsqrt(variance + EPSILON)
    gain = gain_ref[...].reshape(1, C)
    bias = bias_ref[...].reshape(1, C)

    for s in range(1, 8):
        sender = rem(fr - s + 8, 8)
        pltpu.make_async_remote_copy(
            xr.at[sender], xr.at[sender], x_send.at[s], x_recv.at[s],
            device_id=(dp, sender), device_id_type=MESH,
        ).wait_recv()
        copy = pltpu.make_async_remote_copy(
            ts.at[s], tr.at[fr], t_send.at[s], t_recv.at[s],
            device_id=(dp, rem(fr + s, 8)), device_id_type=MESH,
        )
        copy.start()
        sends.append(copy)

    cell_row = rem(lax.broadcasted_iota(jnp.int32, (BLOCK, C), 0), 8)

    def valid_of(j):
        outside = ((j == 0) & (fr == 0)) | ((j == WIDE - 1) & (fr == FRAMES - 1))
        return 1.0 - outside.astype(F32)

    def sigmoid(v):
        return 0.5 * jnp.tanh(0.5 * v) + 0.5

    def store_row_shifts(ref, at, value, first, last):
        ref[at, first * C : (first + 1) * C] = jnp.where(
            cell_row == 0, 0.0, pltpu.roll(value, 1, 0)
        ).astype(BF16)
        ref[at, C : 2 * C] = value.astype(BF16)
        ref[at, last * C : (last + 1) * C] = jnp.where(
            cell_row == 7, 0.0, pltpu.roll(value, BLOCK - 1, 0)
        ).astype(BF16)

    def hidden_body(n, carry):
        p = div(n, WIDE // 2)
        jj = rem(n, WIDE // 2)
        at = pl.ds(pl.multiple_of(jj * 16, 16), 16)
        even = xr[2 * p, at].astype(F32)
        odd = xr[2 * p + 1, at].astype(F32)
        for h in range(2):
            j = 2 * jj + h
            v = jnp.concatenate([even[8 * h : 8 * h + 8], odd[8 * h : 8 * h + 8]], axis=0)
            normed = (v - mean) * inverse * gain + bias
            value = normed * sigmoid(normed) * valid_of(j)
            dst = pl.ds(pl.multiple_of(j * SLAB + p * 16, 16), 16)
            xj[dst, :] = v.astype(BF16)
            store_row_shifts(hid, dst, value, 0, 2)
        return carry

    lax.fori_loop(0, 4 * (WIDE // 2), hidden_body, 0)

    def pair_copy(src, dst, n):
        return pltpu.make_async_remote_copy(
            src, dst, pair_send.at[n], pair_recv.at[n], device_id=partner, device_id_type=MESH
        )

    pad8 = jnp.zeros((8, C), F32)

    def store_frame_shifts(ref, at, value, before, after):
        ref[at, before * C : (before + 1) * C] = jnp.concatenate(
            [pad8, value[: SLAB - 8]], axis=0
        ).astype(BF16)
        ref[at, C : 2 * C] = value.astype(BF16)
        ref[at, after * C : (after + 1) * C] = jnp.concatenate(
            [value[8:], pad8], axis=0
        ).astype(BF16)

    def rows_of(b):
        return pl.ds(pl.multiple_of(b * 256, 256), 256)

    def hidden_pair(m, lanes=pl.ds(0, CELLS)):
        src = pl.ds(pl.multiple_of(720 * m + 352 * (1 - core), 16), 384)
        return pltpu.make_async_remote_copy(
            hid_t.at[src, lanes], hid_p.at[m, :, lanes], hp_send.at[m], hp_recv.at[m],
            device_id=partner, device_id_type=MESH,
        )

    for copy in w_copies:
        copy.wait()

    def forward_body(b, carry):
        total = None
        for c in range(3):
            src = pl.ds(pl.multiple_of(b * 256 + c * SLAB, 64), 256)
            part = jnp.dot(hid[src, :], w[c], preferred_element_type=F32)
            total = part if total is None else total + part
            for a in range(3):
                top = (a * 3 + c) * C
                for half in range(2):
                    src = pl.ds(pl.multiple_of(b * 256 + c * SLAB + half * 128, 64), 128)
                    dst = pl.ds(pl.multiple_of(b * 256 + half * 128, 128), 128)
                    hid_t[top : top + C, dst] = hid[src, a * C : (a + 1) * C].T

        def hidden_send(n, carry):
            hidden_pair(rem(me.group + 1 + n, 8), rows_of(b)).start()
            return carry

        lax.fori_loop(0, 8, hidden_send, 0)
        for k in range(4):
            at = pl.ds(pl.multiple_of(b * 256 + k * SLAB, SLAB), SLAB)
            store_frame_shifts(s3, at, total[k * SLAB : (k + 1) * SLAB], 0, 2)
        put(rows_of(b), jnp.dot(s3[rows_of(b), :], wt[...], preferred_element_type=F32))
        for t in range(3):
            for half in range(2):
                at = pl.ds(pl.multiple_of(b * 256 + half * 128, 128), 128)
                s3_t[t * C : (t + 1) * C, at] = s3[at, t * C : (t + 1) * C].T
        for m in range(8):
            src = pl.ds(pl.multiple_of(240 * m + 112 * (1 - core), 16), 144)
            pair_copy(s3_t.at[src, rows_of(b)], s3_p.at[m, :, rows_of(b)], 2).start()
        return carry

    lax.fori_loop(0, 3, forward_body, 0)

    for s in range(1, 8):
        sender = rem(fr - s + 8, 8)
        pltpu.make_async_remote_copy(
            tr.at[sender], tr.at[sender], t_send.at[s], t_recv.at[s],
            device_id=(dp, sender), device_id_type=MESH,
        ).wait_recv()

    scale = float(16 * FRAMES * ROWS * COLS) ** (-0.5)

    def nt(lhs, rhs):
        return lax.dot_general(lhs, rhs, (((1,), (1,)), ((), ())), preferred_element_type=F32)

    def backward_body(b, loss):
        for half in range(2):
            jj = 2 * b + half
            at = pl.ds(pl.multiple_of(jj * 16, 16), 16)
            target = [tr[f, at].astype(F32) for f in range(FRAMES)]
            for h in range(2):
                j = 2 * jj + h
                own = pl.ds(pl.multiple_of(j * SLAB, SLAB), SLAB)
                wide_at = pl.ds(pl.multiple_of((j + 1) * SLAB, SLAB), SLAB)
                taught = jnp.concatenate([t[8 * h : 8 * h + 8] for t in target], axis=0)
                out = get(own).astype(BF16).astype(F32)
                error = xj[wide_at, :].astype(F32) + out - taught
                grad = error * scale
                go[0, own, :] = grad.astype(BF16)
                store_frame_shifts(g3, own, grad, 2, 0)
                loss = loss + jnp.sum((error * error).reshape(FRAMES, 8, C), axis=0)
        src = rows_of(b)
        pair_copy(go.at[0, src], go.at[1, src], 1).start()
        total = None
        for t in range(3):
            part = nt(g3[src, t * C : (t + 1) * C], wt[t * C : (t + 1) * C, :])
            total = part if total is None else total + part
        for k in range(16):
            at = pl.ds(pl.multiple_of(b * 256 + 16 * k, 16), 16)
            value = total[16 * k : 16 * k + 16]
            gs[0, at, :] = value.astype(BF16)
            store_row_shifts(gs3, at, value, 2, 0)
        pair_copy(gs.at[0, src], gs.at[1, src], 3).start()
        return loss

    loss = lax.fori_loop(0, 3, backward_body, jnp.zeros((8, C), F32))

    def wait_pair(dst, n):
        pair_copy(dst, dst, n).wait_recv()

    wait_pair(go.at[1], 1)
    wait_pair(s3_p, 2)

    def time_body(n, carry):
        own = jnp.concatenate(
            [
                s3_t[pl.ds(pl.multiple_of(240 * (4 * n + k) + 112 * core, 16), 144), :]
                for k in range(4)
            ],
            axis=0,
        )
        other = s3_p[pl.ds(4 * n, 4)].reshape(576, CELLS)
        out = jnp.dot(own, go[0], preferred_element_type=F32)
        put(pl.ds(0, 576), out + jnp.dot(other, go[1], preferred_element_type=F32))
        for k in range(4):
            for q in range(8):
                cut = 15 * q % 8
                at = pl.ds(pl.multiple_of(144 * k + 15 * q - cut + 8 * core, 8), 24)
                rows = get(at)[cut : cut + 16].astype(BF16)
                zz, xl = q // 2, q % 2
                stage[3][4 * n + k, xl * 4 + zz] = rows[:, 0:256]
                stage[4][4 * n + k, q] = rows[:, 256:512]
                stage[5][4 * n + k, q] = rows[:, 512:C]
        return carry

    lax.fori_loop(0, 2, time_body, 0)

    def first_send(u, src, step, dst, device):
        pltpu.make_async_remote_copy(
            src, dst, r1_send.at[u, step - 1], r1_recv.at[u, step - 1],
            device_id=device, device_id_type=MESH,
        ).start()

    def send_y(u, m):
        mx, my = div(m, 4), rem(m, 4)
        step = rem(my - me.y + 4, 4)

        @pl.when(step != 0)
        def _():
            first_send(
                u, stage[u].at[m], step,
                r1[u].at[step - 1, pl.ds(mx * 8, 8)],
                (me.dp_x[0] + 2 * my + core, fr),
            )

    def send_z(u, m):
        for s in range(1, 4):
            first_send(
                u, stage[u].at[m, pl.ds(me.fr_z[s], 2)], s,
                r1[u].at[s - 1, pl.ds(m * 2, 2)], me.along_axis(2, s),
            )

    def send_x(u, m):
        mx, my = div(m, 4), rem(m, 4)
        for xl in range(2):
            there = 2 * mx + xl
            step = rem(there - me.x + 4, 4)

            @pl.when(step != 0)
            def _():
                first_send(
                    u, stage[u].at[m, pl.ds(xl * 4, 4)], step,
                    r1[u].at[step - 1, pl.ds(my * 4, 4)],
                    (mx * 8 + me.dp_y[0] + core, me.fr_z[0] + xl),
                )

    def time_send(n, carry):
        m = rem(me.group + 1 + n, 8)
        send_x(3, m)
        send_y(4, m)
        send_z(5, m)
        return carry

    lax.fori_loop(0, 8, time_send, 0)

    wait_pair(gs.at[1], 3)

    def space_body(n, carry):
        m = rem(me.group + 1 + n, 8)
        hidden_pair(m).wait_recv()
        own = hid_t[pl.ds(pl.multiple_of(720 * m + 352 * core, 16), 384), :]
        out = jnp.dot(own, gs[0], preferred_element_type=F32)
        put(pl.ds(0, 384), out + jnp.dot(hid_p[m], gs[1], preferred_element_type=F32))
        for q in range(8):
            cut = 45 * q % 8
            at = pl.ds(pl.multiple_of(45 * q - cut + 8 * core, 8), 56)
            rows = get(at)[cut : cut + 48].astype(BF16)
            zz, xl = q // 2, q % 2
            stage[0][m, q] = rows[0:16]
            stage[1][m, q] = rows[16:32]
            stage[2][m, xl * 4 + zz] = rows[32:48]
        send_z(0, m)
        send_y(1, m)
        send_x(2, m)
        return carry

    lax.fori_loop(0, 8, space_body, 0)

    def clear_body(b, carry):
        put(pl.ds(pl.multiple_of(b * SLAB, SLAB), SLAB), jnp.zeros((SLAB, C), F32))
        return carry

    lax.fori_loop(0, WIDE, clear_body, 0)

    def grad_hidden(c):
        def body(b, carry):
            src = pl.ds(pl.multiple_of(b * 256, 256), 256)
            dst = pl.ds(pl.multiple_of(b * 256 + c * SLAB, 64), 256)
            total = get(dst)
            for a in range(3):
                total = total + nt(gs3[src, a * C : (a + 1) * C], w[c, a * C : (a + 1) * C, :])
            put(dst, total)
            return carry

        lax.fori_loop(0, 3, body, 0)

    def first_steps(u, wait):
        for s in range(1, 4):
            copy = pltpu.make_async_remote_copy(
                r1[u].at[s - 1], r1[u].at[s - 1], r1_send.at[u, s - 1], r1_recv.at[u, s - 1],
                device_id=me.along_axis(0, 1), device_id_type=MESH,
            )
            if wait == "recv":
                copy.wait_recv()
            else:
                copy.wait_send()

    def plane_copy(u, src, dst, device):
        return pltpu.make_async_remote_copy(
            src, dst, r2_send.at[u], r2_recv.at[u], device_id=device, device_id_type=MESH
        )

    def plane_all(u):
        return plane_copy(u, r2[u], r2[u], me.along_axis(0, 1))

    def second_phase(u):
        first_steps(u, "recv")
        axis, one, two = AXES[u]
        for step_one in range(4):
            for step_two in range(4):
                n = step_one * 4 + step_two
                if axis == 2:
                    x_half, xl, y = div(me.dp_x[step_one], 8), me.fr_x[step_one], me.at[1][step_two]
                    k = x_half * 8 + y * 2 + xl
                    own = stage[u][x_half * 4 + y, me.fr_z[0] + xl]
                elif axis == 0:
                    y, z = me.at[1][step_one], me.at[2][step_two]
                    k = y * 4 + z
                    own = stage[u][me.xh * 4 + y, me.xl * 4 + z]
                else:
                    q = me.fr_z[step_one] + me.fr_x[step_two]
                    k = me.dp_x[step_two] + q
                    own = stage[u][div(me.dp_x[step_two], 2) + me.y, q]
                total = own.astype(F32)
                for s in range(3):
                    total = total + r1[u][s, k].astype(F32)
                p2[u][n] = total.astype(BF16)
                if n > 0:
                    plane_copy(
                        u, p2[u].at[n], r2[u].at[n - 1],
                        me.in_plane(one, step_one, two, step_two),
                    ).start()

    def last_phase(u):
        plane_all(u).wait_recv()
        total = p2[u][0].astype(F32)
        for n in range(15):
            total = total + r2[u][n].astype(F32)
        low, high = LANES[u]
        top = min(u, 3) * BLOCK
        rows_out[top : top + BLOCK, low:high] = total

    grad_hidden(0)
    for u in range(3, 6):
        second_phase(u)
    grad_hidden(1)
    grad_hidden(2)

    def norm_body(n, carry):
        gain_sum, bias_sum = carry
        at = pl.ds(pl.multiple_of(n * 16, 16), 16)
        centred = (xj[at, :].astype(F32) - mean) * inverse
        normed = centred * gain + bias
        s = sigmoid(normed)
        grad = get(at) * s * (1.0 + normed * (1.0 - s)) * valid_of(div(n, 4))
        weighted = grad * centred
        return (gain_sum + weighted[0:8] + weighted[8:16], bias_sum + grad[0:8] + grad[8:16])

    gain_sum, bias_sum = lax.fori_loop(0, CELLS_WIDE // 16, norm_body, (zero, zero))
    at_plane = me.x * 4 + me.z
    small_a[at_plane, 0:1] = jnp.sum(gain_sum, axis=0, keepdims=True)
    small_a[at_plane, 1:2] = jnp.sum(bias_sum, axis=0, keepdims=True)
    small_a[at_plane, 2:3] = jnp.sum(loss, axis=0, keepdims=True)
    small_a[at_plane, 3:8] = jnp.zeros((5, C), F32)

    for n in range(1, 16):
        pltpu.make_async_remote_copy(
            small_a.at[at_plane], small_a.at[at_plane], a_send, a_recv,
            device_id=me.in_plane(0, n // 4, 2, n % 4), device_id_type=MESH,
        ).start()

    for u in range(3):
        second_phase(u)

    small_all = pltpu.make_async_remote_copy(
        small_a.at[pl.ds(0, 15)], small_a.at[pl.ds(0, 15)], a_send, a_recv,
        device_id=partner, device_id_type=MESH,
    )
    small_all.wait_recv()
    total = small_a[0]
    for f in range(1, 16):
        total = total + small_a[f]
    at_rest = me.y * 2 + core
    small_b[at_rest] = total
    for s in range(4):
        for t in range(2):
            if s + t > 0:
                to = (me.dp_x[0] + me.dp_y[s] + core + t * across, fr)
                pltpu.make_async_remote_copy(
                    small_b.at[at_rest], small_b.at[at_rest], b_send, b_recv,
                    device_id=to, device_id_type=MESH,
                ).start()

    for u in range(3, 6):
        last_phase(u)

    rest_all = pltpu.make_async_remote_copy(
        small_b.at[pl.ds(0, 7)], small_b.at[pl.ds(0, 7)], b_send, b_recv,
        device_id=partner, device_id_type=MESH,
    )
    rest_all.wait_recv()
    total = small_b[0]
    for d in range(1, 8):
        total = total + small_b[d]
    small_out[...] = total

    for u in range(3):
        last_phase(u)

    for copy in sends:
        copy.wait_send()
    small_all.wait_send()
    rest_all.wait_send()
    for m in range(8):
        hidden_pair(m).wait_send()
    pair_copy(go.at[0], go.at[1], 1).wait_send()
    pair_copy(s3_p, s3_p, 2).wait_send()
    pair_copy(gs.at[0], gs.at[1], 3).wait_send()
    for u in range(UNITS):
        first_steps(u, "send")
        plane_all(u).wait_send()


def finish(rows, small, space, time, gain, bias, loss):
    space[...] = rows[0:45]
    time[...] = rows[48:63]
    gain[...] = small[0]
    bias[...] = small[1]
    loss[0, 0] = jnp.sum(small[2:3]) / float(16 * FRAMES * ROWS * COLS * C)


def shards(clips_in, teacher, spatial_weight, temporal_weight, norm_gain, norm_bias):
    vmem = pl.BlockSpec(memory_space=pltpu.VMEM)
    hbm = pl.BlockSpec(memory_space=pl.ANY)
    dma = pltpu.SemaphoreType.DMA
    wide = [high - low for low, high in LANES]
    rows, small = pl.pallas_call(
        kernel,
        out_shape=(
            jax.ShapeDtypeStruct((64, C), F32),
            jax.ShapeDtypeStruct((8, C), F32),
        ),
        in_specs=[hbm, hbm, vmem, vmem, hbm, hbm],
        out_specs=(vmem, vmem),
        scratch_shapes=[
            pltpu.VMEM((3, 3 * C, C), BF16),
            pltpu.VMEM((3 * C, C), BF16),
            pltpu.VMEM((ROWS, COLS, C), BF16),
            pltpu.VMEM((ROWS, COLS, C), BF16),
            pltpu.VMEM((FRAMES, WIDE * ROWS, C), BF16),
            pltpu.VMEM((FRAMES, OWN * ROWS, C), BF16),
            pltpu.VMEM((FRAMES, WIDE * ROWS, C), BF16),
            pltpu.VMEM((FRAMES, OWN * ROWS, C), BF16),
            pltpu.VMEM((FRAMES, 16, C), F32),
            pltpu.VMEM((CELLS_WIDE, 3 * C), BF16),
            pltpu.VMEM((9 * C + 48, CELLS), BF16),
            pltpu.VMEM((8, 384, CELLS), BF16),
            pltpu.VMEM((CELLS, 3 * C), BF16),
            pltpu.VMEM((3 * C + 16, CELLS), BF16),
            pltpu.VMEM((8, 144, CELLS), BF16),
            pltpu.VMEM((2, CELLS, C), BF16),
            pltpu.VMEM((2, CELLS, C), BF16),
            pltpu.VMEM((CELLS_WIDE, C), BF16),
            pltpu.VMEM((TILES, CELLS_WIDE, 128), F32),
            *[pltpu.VMEM((8, 8, BLOCK, n), BF16) for n in wide],
            *[pltpu.VMEM((3, 16, BLOCK, n), BF16) for n in wide],
            *[pltpu.VMEM((16, BLOCK, n), BF16) for n in wide],
            *[pltpu.VMEM((15, BLOCK, n), BF16) for n in wide],
            pltpu.VMEM((16, 8, C), F32),
            pltpu.VMEM((8, 8, C), F32),
            dma((10,)),
            dma((2,)),
            dma((8,)), dma((8,)),
            dma((8,)), dma((8,)),
            dma((8,)), dma((8,)),
            dma((4,)), dma((4,)),
            dma((8,)), dma((8,)),
            dma((UNITS, 3)), dma((UNITS, 3)),
            dma((UNITS,)), dma((UNITS,)),
            dma, dma,
            dma, dma,
        ],
        compiler_params=pltpu.CompilerParams(
            collective_id=0, has_side_effects=True, vmem_limit_bytes=64 * 2**20 - 2**17
        ),
    )(
        clips_in.reshape(ROWS, COLS, C), teacher.reshape(ROWS, COLS, C), norm_gain, norm_bias,
        spatial_weight, temporal_weight.reshape(3 * C, C),
    )
    spatial_grad, temporal_grad, gain_grad, bias_grad, loss = pl.pallas_call(
        finish,
        out_shape=(
            jax.ShapeDtypeStruct((45, C), F32),
            jax.ShapeDtypeStruct((15, C), F32),
            jax.ShapeDtypeStruct((C,), F32),
            jax.ShapeDtypeStruct((C,), F32),
            jax.ShapeDtypeStruct((1, 1), F32),
        ),
        in_specs=[vmem, vmem],
        out_specs=(vmem, vmem, vmem, vmem, pl.BlockSpec(memory_space=pltpu.SMEM)),
    )(rows, small)
    return (spatial_grad, temporal_grad, gain_grad, bias_grad, loss.reshape(()))


def solution(mesh):
    return jax.shard_map(
        shards,
        mesh=mesh,
        in_specs=(
            P("dp", "frame", None, None, None),
            P("dp", "frame", None, None, None),
            P(),
            P(),
            P(),
            P(),
        ),
        out_specs=(P(("dp", "frame"), None), P(("dp", "frame"), None), P(), P(), P()),
        check_vma=False,
    )
```

```python
import jax
import jax.numpy as jnp
from jax import lax
from jax.experimental import pallas as pl
from jax.experimental.pallas import tpu as pltpu
from jax.sharding import PartitionSpec as P

GROUPS = 32
EPSILON = 1e-05
F32 = jnp.float32
BF16 = jnp.bfloat16
MESH = pl.DeviceIdType.MESH

FRAMES = 8
ROWS = 8
COLS = 96
C = 640
OWN = COLS // FRAMES
WIDE = OWN + 2
CELLS = OWN * FRAMES * ROWS
CELLS_WIDE = WIDE * FRAMES * ROWS
SLAB = FRAMES * ROWS
BLOCK = 16
TILES = C // 128
AXES = ((2, 0, 1), (1, 2, 0), (0, 1, 2), (0, 1, 2), (1, 2, 0), (2, 0, 1))
LANES = ((0, C), (0, C), (0, C), (0, 256), (256, 512), (512, C))
UNITS = 6


def rem(a, b):
    return lax.rem(a, jnp.int32(b))


def div(a, b):
    return lax.div(a, jnp.int32(b))


class Place:
    def __init__(self):
        self.dp = lax.axis_index("dp")
        self.fr = lax.axis_index("frame")
        self.core = rem(self.dp, 2)
        self.y = rem(div(self.dp, 2), 4)
        self.xh = div(self.dp, 8)
        self.z = div(self.fr, 2)
        self.xl = rem(self.fr, 2)
        self.x = 2 * self.xh + self.xl
        self.group = self.xh * 4 + self.y
        self.along = (self.x, self.y, self.z)

        self.at = [[rem(v + step, 4) for step in range(4)] for v in self.along]
        self.dp_x = [div(v, 2) * 8 for v in self.at[0]]
        self.fr_x = [rem(v, 2) for v in self.at[0]]
        self.dp_y = [2 * v for v in self.at[1]]
        self.fr_z = [2 * v for v in self.at[2]]

    def further(self, *steps):
        x, y, z = steps
        return (self.dp_x[x] + self.dp_y[y] + self.core, self.fr_z[z] + self.fr_x[x])

    def along_axis(self, axis, step):
        return self.further(*(step if axis == n else 0 for n in range(3)))

    def in_plane(self, one, step_one, two, step_two):
        return self.further(
            *(step_one if n == one else step_two if n == two else 0 for n in range(3))
        )


def kernel(
    x_hbm, t_hbm, gain_ref, bias_ref, w_hbm, wt_hbm,
    rows_out, small_out,
    w, wt, xraw, traw, xs, ts, xr, tr, stats, hid, hid_t, hid_p, s3, s3_t, s3_p, go, gs, xj, acc,
    stage0, stage1, stage2, stage3, stage4, stage5,
    r10, r11, r12, r13, r14, r15,
    p20, p21, p22, p23, p24, p25,
    r20, r21, r22, r23, r24, r25,
    small_a, small_b,
    w_sem, own_sem, x_send, x_recv, t_send, t_recv, st_send, st_recv, pair_send, pair_recv,
    hp_send, hp_recv, r1_send, r1_recv, r2_send, r2_recv, a_send, a_recv, b_send, b_recv,
):
    me = Place()
    dp, fr, core = me.dp, me.fr, me.core
    gs3 = s3
    g3 = hid
    stage = (stage0, stage1, stage2, stage3, stage4, stage5)
    r1 = (r10, r11, r12, r13, r14, r15)
    p2 = (p20, p21, p22, p23, p24, p25)
    r2 = (r20, r21, r22, r23, r24, r25)

    def get(at):
        return jnp.concatenate([acc[l, at, :] for l in range(TILES)], axis=1)

    def put(at, value):
        for l in range(TILES):
            acc[l, at, :] = value[:, l * 128 : (l + 1) * 128]

    load_x = pltpu.make_async_copy(x_hbm, xraw, own_sem.at[0])
    load_x.start()
    load_t = pltpu.make_async_copy(t_hbm, traw, own_sem.at[1])
    load_t.start()

    w_copies = []
    for a in range(3):
        for c in range(3):
            w_copies.append(
                pltpu.make_async_copy(
                    w_hbm.at[a, c], w.at[c, pl.ds(a * C, C)], w_sem.at[3 * a + c]
                )
            )
    w_copies.append(pltpu.make_async_copy(wt_hbm, wt, w_sem.at[9]))
    for copy in w_copies:
        copy.start()

    barrier = pltpu.get_barrier_semaphore()

    def greet(device):
        pl.semaphore_signal(barrier, inc=1, device_id=device, device_id_type=MESH)

    for axis in range(3):
        for s in range(1, 4):
            greet(me.along_axis(axis, s))
    for one, two in ((0, 1), (1, 2), (0, 2)):
        for s in range(1, 4):
            for t in range(1, 4):
                greet(me.in_plane(one, s, two, t))
    across = 1 - 2 * core
    for s in range(4):
        greet((me.dp_x[0] + me.dp_y[s] + core + across, fr))
    partner = (dp + across, fr)

    load_x.wait()

    def moment_body(i, carry):
        total, square = carry
        v = xraw[i].astype(F32)
        put(pl.ds(pl.multiple_of(i * COLS, 8), COLS), v)
        v = v.reshape(COLS // 8, 8, C)
        return (total + jnp.sum(v, axis=0), square + jnp.sum(v * v, axis=0))

    zero = jnp.zeros((8, C), F32)
    total, square = lax.fori_loop(0, ROWS, moment_body, (zero, zero))
    stats[fr, 0:8] = total
    stats[fr, 8:16] = square

    pl.semaphore_wait(barrier, 40)

    sends = []
    for s in range(1, 8):
        to = rem(fr + s, 8)
        copy = pltpu.make_async_remote_copy(
            stats.at[fr], stats.at[fr], st_send.at[s], st_recv.at[s],
            device_id=(dp, to), device_id_type=MESH,
        )
        copy.start()
        sends.append(copy)

    def two_columns(first, second):
        return jnp.concatenate(
            [
                jnp.concatenate(
                    [acc[l, pl.ds(j, ROWS, stride=COLS), :] for l in range(TILES)], axis=1
                )
                for j in (first, second)
            ],
            axis=0,
        ).astype(BF16)

    def x_share(ref, to):
        def body(jj, carry):
            j = OWN * to - 1 + 2 * jj
            ref[pl.ds(pl.multiple_of(16 * jj, 16), 16), :] = two_columns(
                jnp.maximum(j, 0), jnp.minimum(j + 1, COLS - 1)
            )
            return carry

        lax.fori_loop(0, WIDE // 2, body, 0)

    def t_share(ref, to):
        def body(jj, carry):
            j = OWN * to + 2 * jj
            ref[pl.ds(pl.multiple_of(16 * jj, 16), 16), :] = two_columns(j, j + 1)
            return carry

        lax.fori_loop(0, OWN // 2, body, 0)

    for s in range(1, 8):
        to = rem(fr + s, 8)
        x_share(xs.at[s], to)
        copy = pltpu.make_async_remote_copy(
            xs.at[s], xr.at[fr], x_send.at[s], x_recv.at[s],
            device_id=(dp, to), device_id_type=MESH,
        )
        copy.start()
        sends.append(copy)
    x_share(xr.at[fr], fr)

    load_t.wait()

    def teacher_body(i, carry):
        put(pl.ds(pl.multiple_of(i * COLS, 8), COLS), traw[i].astype(F32))
        return carry

    lax.fori_loop(0, ROWS, teacher_body, 0)
    for s in range(1, 8):
        to = rem(fr + s, 8)
        t_share(ts.at[s], to)
    t_share(tr.at[fr], fr)

    hid_t[9 * C :, :] = jnp.zeros((48, CELLS), BF16)
    s3_t[3 * C :, :] = jnp.zeros((16, CELLS), BF16)

    row = lax.broadcasted_iota(jnp.int32, (C, C), 0)
    col = lax.broadcasted_iota(jnp.int32, (C, C), 1)
    same = (
        lax.shift_right_logical(row * 3277, 16) == lax.shift_right_logical(col * 3277, 16)
    ).astype(F32).astype(BF16)
    for s in range(1, 8):
        sender = rem(fr - s + 8, 8)
        pltpu.make_async_remote_copy(
            stats.at[sender], stats.at[sender], st_send.at[s], st_recv.at[s],
            device_id=(dp, sender), device_id_type=MESH,
        ).wait_recv()
    moments = stats[0]
    for f in range(1, FRAMES):
        moments = moments + stats[f]
    high = moments.astype(BF16)
    rest = moments - high.astype(F32)
    middle = rest.astype(BF16)
    low = (rest - middle.astype(F32)).astype(BF16)
    wide = (
        jnp.dot(high, same, preferred_element_type=F32)
        + jnp.dot(middle, same, preferred_element_type=F32)
        + jnp.dot(low, same, preferred_element_type=F32)
    )
    size = float(FRAMES * ROWS * COLS * (C // GROUPS))
    mean = jnp.sum(wide[0:8], axis=0, keepdims=True) / size
    variance = jnp.sum(wide[8:16], axis=0, keepdims=True) / size - mean * mean
    inverse = lax.rsqrt(variance + EPSILON)
    gain = gain_ref[...].reshape(1, C)
    bias = bias_ref[...].reshape(1, C)

    for s in range(1, 8):
        sender = rem(fr - s + 8, 8)
        pltpu.make_async_remote_copy(
            xr.at[sender], xr.at[sender], x_send.at[s], x_recv.at[s],
            device_id=(dp, sender), device_id_type=MESH,
        ).wait_recv()
        copy = pltpu.make_async_remote_copy(
            ts.at[s], tr.at[fr], t_send.at[s], t_recv.at[s],
            device_id=(dp, rem(fr + s, 8)), device_id_type=MESH,
        )
        copy.start()
        sends.append(copy)

    cell_row = rem(lax.broadcasted_iota(jnp.int32, (BLOCK, C), 0), 8)

    def valid_of(j):
        outside = ((j == 0) & (fr == 0)) | ((j == WIDE - 1) & (fr == FRAMES - 1))
        return 1.0 - outside.astype(F32)

    def sigmoid(v):
        return 0.5 * jnp.tanh(0.5 * v) + 0.5

    def store_row_shifts(ref, at, value, first, last):
        ref[at, first * C : (first + 1) * C] = jnp.where(
            cell_row == 0, 0.0, pltpu.roll(value, 1, 0)
        ).astype(BF16)
        ref[at, C : 2 * C] = value.astype(BF16)
        ref[at, last * C : (last + 1) * C] = jnp.where(
            cell_row == 7, 0.0, pltpu.roll(value, BLOCK - 1, 0)
        ).astype(BF16)

    def hidden_body(n, carry):
        p = div(n, WIDE // 2)
        jj = rem(n, WIDE // 2)
        at = pl.ds(pl.multiple_of(jj * 16, 16), 16)
        even = xr[2 * p, at].astype(F32)
        odd = xr[2 * p + 1, at].astype(F32)
        for h in range(2):
            j = 2 * jj + h
            v = jnp.concatenate([even[8 * h : 8 * h + 8], odd[8 * h : 8 * h + 8]], axis=0)
            normed = (v - mean) * inverse * gain + bias
            value = normed * sigmoid(normed) * valid_of(j)
            dst = pl.ds(pl.multiple_of(j * SLAB + p * 16, 16), 16)
            xj[dst, :] = v.astype(BF16)
            store_row_shifts(hid, dst, value, 0, 2)
        return carry

    lax.fori_loop(0, 4 * (WIDE // 2), hidden_body, 0)

    def pair_copy(src, dst, n):
        return pltpu.make_async_remote_copy(
            src, dst, pair_send.at[n], pair_recv.at[n], device_id=partner, device_id_type=MESH
        )

    pad8 = jnp.zeros((8, C), F32)

    def store_frame_shifts(ref, at, value, before, after):
        ref[at, before * C : (before + 1) * C] = jnp.concatenate(
            [pad8, value[: SLAB - 8]], axis=0
        ).astype(BF16)
        ref[at, C : 2 * C] = value.astype(BF16)
        ref[at, after * C : (after + 1) * C] = jnp.concatenate(
            [value[8:], pad8], axis=0
        ).astype(BF16)

    def rows_of(b):
        return pl.ds(pl.multiple_of(b * 256, 256), 256)

    def hidden_pair(m, lanes=pl.ds(0, CELLS)):
        src = pl.ds(pl.multiple_of(720 * m + 352 * (1 - core), 16), 384)
        return pltpu.make_async_remote_copy(
            hid_t.at[src, lanes], hid_p.at[m, :, lanes], hp_send.at[m], hp_recv.at[m],
            device_id=partner, device_id_type=MESH,
        )

    for copy in w_copies:
        copy.wait()

    def forward_body(b, carry):
        windows = [
            hid[pl.ds(pl.multiple_of(b * 256 + c * SLAB, 64), 256), :] for c in range(3)
        ]
        total = jnp.dot(
            jnp.concatenate(windows, axis=1), w[...].reshape(9 * C, C),
            preferred_element_type=F32,
        )
        for c in range(3):
            for a in range(3):
                top = (a * 3 + c) * C
                for half in range(2):
                    src = pl.ds(pl.multiple_of(b * 256 + c * SLAB + half * 128, 64), 128)
                    dst = pl.ds(pl.multiple_of(b * 256 + half * 128, 128), 128)
                    hid_t[top : top + C, dst] = hid[src, a * C : (a + 1) * C].T

        def hidden_send(n, carry):
            hidden_pair(rem(me.group + 1 + n, 8), rows_of(b)).start()
            return carry

        lax.fori_loop(0, 8, hidden_send, 0)
        for k in range(4):
            at = pl.ds(pl.multiple_of(b * 256 + k * SLAB, SLAB), SLAB)
            store_frame_shifts(s3, at, total[k * SLAB : (k + 1) * SLAB], 0, 2)
        put(rows_of(b), jnp.dot(s3[rows_of(b), :], wt[...], preferred_element_type=F32))
        for t in range(3):
            for half in range(2):
                at = pl.ds(pl.multiple_of(b * 256 + half * 128, 128), 128)
                s3_t[t * C : (t + 1) * C, at] = s3[at, t * C : (t + 1) * C].T
        for m in range(8):
            src = pl.ds(pl.multiple_of(240 * m + 112 * (1 - core), 16), 144)
            pair_copy(s3_t.at[src, rows_of(b)], s3_p.at[m, :, rows_of(b)], 2).start()
        return carry

    lax.fori_loop(0, 3, forward_body, 0)

    for s in range(1, 8):
        sender = rem(fr - s + 8, 8)
        pltpu.make_async_remote_copy(
            tr.at[sender], tr.at[sender], t_send.at[s], t_recv.at[s],
            device_id=(dp, sender), device_id_type=MESH,
        ).wait_recv()

    scale = float(16 * FRAMES * ROWS * COLS) ** (-0.5)

    def nt(lhs, rhs):
        return lax.dot_general(lhs, rhs, (((1,), (1,)), ((), ())), preferred_element_type=F32)

    def backward_body(b, loss):
        for half in range(2):
            jj = 2 * b + half
            at = pl.ds(pl.multiple_of(jj * 16, 16), 16)
            target = [tr[f, at].astype(F32) for f in range(FRAMES)]
            for h in range(2):
                j = 2 * jj + h
                own = pl.ds(pl.multiple_of(j * SLAB, SLAB), SLAB)
                wide_at = pl.ds(pl.multiple_of((j + 1) * SLAB, SLAB), SLAB)
                taught = jnp.concatenate([t[8 * h : 8 * h + 8] for t in target], axis=0)
                out = get(own).astype(BF16).astype(F32)
                error = xj[wide_at, :].astype(F32) + out - taught
                grad = error * scale
                go[0, own, :] = grad.astype(BF16)
                store_frame_shifts(g3, own, grad, 2, 0)
                loss = loss + jnp.sum((error * error).reshape(FRAMES, 8, C), axis=0)
        src = rows_of(b)
        pair_copy(go.at[0, src], go.at[1, src], 1).start()
        total = None
        for t in range(3):
            part = nt(g3[src, t * C : (t + 1) * C], wt[t * C : (t + 1) * C, :])
            total = part if total is None else total + part
        for k in range(16):
            at = pl.ds(pl.multiple_of(b * 256 + 16 * k, 16), 16)
            value = total[16 * k : 16 * k + 16]
            gs[0, at, :] = value.astype(BF16)
            store_row_shifts(gs3, at, value, 2, 0)
        pair_copy(gs.at[0, src], gs.at[1, src], 3).start()
        return loss

    loss = lax.fori_loop(0, 3, backward_body, jnp.zeros((8, C), F32))

    def wait_pair(dst, n):
        pair_copy(dst, dst, n).wait_recv()

    wait_pair(go.at[1], 1)
    wait_pair(s3_p, 2)

    def time_body(n, carry):
        own = jnp.concatenate(
            [
                s3_t[pl.ds(pl.multiple_of(240 * (4 * n + k) + 112 * core, 16), 144), :]
                for k in range(4)
            ],
            axis=0,
        )
        other = s3_p[pl.ds(4 * n, 4)].reshape(576, CELLS)
        both = jnp.concatenate([own, other], axis=1)
        out = jnp.dot(both, go[...].reshape(2 * CELLS, C), preferred_element_type=F32)
        put(pl.ds(0, 576), out)
        for k in range(4):
            for q in range(8):
                cut = 15 * q % 8
                at = pl.ds(pl.multiple_of(144 * k + 15 * q - cut + 8 * core, 8), 24)
                rows = get(at)[cut : cut + 16].astype(BF16)
                zz, xl = q // 2, q % 2
                stage[3][4 * n + k, xl * 4 + zz] = rows[:, 0:256]
                stage[4][4 * n + k, q] = rows[:, 256:512]
                stage[5][4 * n + k, q] = rows[:, 512:C]
        return carry

    lax.fori_loop(0, 2, time_body, 0)

    def first_send(u, src, step, dst, device):
        pltpu.make_async_remote_copy(
            src, dst, r1_send.at[u, step - 1], r1_recv.at[u, step - 1],
            device_id=device, device_id_type=MESH,
        ).start()

    def send_y(u, m):
        mx, my = div(m, 4), rem(m, 4)
        step = rem(my - me.y + 4, 4)

        @pl.when(step != 0)
        def _():
            first_send(
                u, stage[u].at[m], step,
                r1[u].at[step - 1, pl.ds(mx * 8, 8)],
                (me.dp_x[0] + 2 * my + core, fr),
            )

    def send_z(u, m):
        for s in range(1, 4):
            first_send(
                u, stage[u].at[m, pl.ds(me.fr_z[s], 2)], s,
                r1[u].at[s - 1, pl.ds(m * 2, 2)], me.along_axis(2, s),
            )

    def send_x(u, m):
        mx, my = div(m, 4), rem(m, 4)
        for xl in range(2):
            there = 2 * mx + xl
            step = rem(there - me.x + 4, 4)

            @pl.when(step != 0)
            def _():
                first_send(
                    u, stage[u].at[m, pl.ds(xl * 4, 4)], step,
                    r1[u].at[step - 1, pl.ds(my * 4, 4)],
                    (mx * 8 + me.dp_y[0] + core, me.fr_z[0] + xl),
                )

    def time_send(n, carry):
        m = rem(me.group + 1 + n, 8)
        send_x(3, m)
        send_y(4, m)
        send_z(5, m)
        return carry

    lax.fori_loop(0, 8, time_send, 0)

    wait_pair(gs.at[1], 3)

    def space_group(n):
        return rem(me.group + 1 + n, 8)

    def space_cut(n):
        m = space_group(n)
        half = rem(n, 2) * 384 + 8 * core
        for q in range(8):
            cut = 45 * q % 8
            at = pl.ds(pl.multiple_of(half + 45 * q - cut, 8), 56)
            rows = get(at)[cut : cut + 48].astype(BF16)
            zz, xl = q // 2, q % 2
            stage[0][m, q] = rows[0:16]
            stage[1][m, q] = rows[16:32]
            stage[2][m, xl * 4 + zz] = rows[32:48]

    def space_send(n):
        m = space_group(n)
        send_z(0, m)
        send_y(1, m)
        send_x(2, m)

    def space_dot(n):
        m = space_group(n)
        own = hid_t[pl.ds(pl.multiple_of(720 * m + 352 * core, 16), 384), :]
        both = jnp.concatenate([own, hid_p[m]], axis=1)
        out = jnp.dot(both, gs[...].reshape(2 * CELLS, C), preferred_element_type=F32)
        put(pl.ds(pl.multiple_of(rem(n, 2) * 384, 128), 384), out)

    hidden_pair(space_group(0)).wait_recv()
    space_dot(0)

    def space_body(n, carry):
        hidden_pair(space_group(n)).wait_recv()
        space_cut(n - 1)
        space_dot(n)
        space_send(n - 1)
        return carry

    lax.fori_loop(1, 8, space_body, 0)
    space_cut(7)
    space_send(7)

    put(pl.ds(CELLS, 2 * SLAB), jnp.zeros((2 * SLAB, C), F32))

    def grad_hidden(c):
        def body(b, carry):
            src = pl.ds(pl.multiple_of(b * 256, 256), 256)
            dst = pl.ds(pl.multiple_of(b * 256 + c * SLAB, 64), 256)
            total = get(dst) if c > 0 else None
            for a in range(3):
                part = nt(gs3[src, a * C : (a + 1) * C], w[c, a * C : (a + 1) * C, :])
                total = part if total is None else total + part
            put(dst, total)
            return carry

        lax.fori_loop(0, 3, body, 0)

    def first_steps(u, wait):
        for s in range(1, 4):
            copy = pltpu.make_async_remote_copy(
                r1[u].at[s - 1], r1[u].at[s - 1], r1_send.at[u, s - 1], r1_recv.at[u, s - 1],
                device_id=me.along_axis(0, 1), device_id_type=MESH,
            )
            if wait == "recv":
                copy.wait_recv()
            else:
                copy.wait_send()

    def plane_copy(u, src, dst, device):
        return pltpu.make_async_remote_copy(
            src, dst, r2_send.at[u], r2_recv.at[u], device_id=device, device_id_type=MESH
        )

    def plane_all(u):
        return plane_copy(u, r2[u], r2[u], me.along_axis(0, 1))

    def second_phase(u):
        first_steps(u, "recv")
        axis, one, two = AXES[u]
        for step_one in range(4):
            for step_two in range(4):
                n = step_one * 4 + step_two
                if axis == 2:
                    x_half, xl, y = div(me.dp_x[step_one], 8), me.fr_x[step_one], me.at[1][step_two]
                    k = x_half * 8 + y * 2 + xl
                    own = stage[u][x_half * 4 + y, me.fr_z[0] + xl]
                elif axis == 0:
                    y, z = me.at[1][step_one], me.at[2][step_two]
                    k = y * 4 + z
                    own = stage[u][me.xh * 4 + y, me.xl * 4 + z]
                else:
                    q = me.fr_z[step_one] + me.fr_x[step_two]
                    k = me.dp_x[step_two] + q
                    own = stage[u][div(me.dp_x[step_two], 2) + me.y, q]
                total = own.astype(F32)
                for s in range(3):
                    total = total + r1[u][s, k].astype(F32)
                p2[u][n] = total.astype(BF16)
                if n > 0:
                    plane_copy(
                        u, p2[u].at[n], r2[u].at[n - 1],
                        me.in_plane(one, step_one, two, step_two),
                    ).start()

    def last_phase(u):
        plane_all(u).wait_recv()
        total = p2[u][0].astype(F32)
        for n in range(15):
            total = total + r2[u][n].astype(F32)
        low, high = LANES[u]
        top = min(u, 3) * BLOCK
        rows_out[top : top + BLOCK, low:high] = total

    grad_hidden(0)
    for u in range(3, 6):
        second_phase(u)
    grad_hidden(1)
    grad_hidden(2)

    def norm_body(n, carry):
        gain_sum, bias_sum = carry
        at = pl.ds(pl.multiple_of(n * 16, 16), 16)
        centred = (xj[at, :].astype(F32) - mean) * inverse
        normed = centred * gain + bias
        s = sigmoid(normed)
        grad = get(at) * s * (1.0 + normed * (1.0 - s)) * valid_of(div(n, 4))
        weighted = grad * centred
        return (gain_sum + weighted[0:8] + weighted[8:16], bias_sum + grad[0:8] + grad[8:16])

    gain_sum, bias_sum = lax.fori_loop(0, CELLS_WIDE // 16, norm_body, (zero, zero), unroll=2)
    at_plane = me.x * 4 + me.z
    small_a[at_plane, 0:1] = jnp.sum(gain_sum, axis=0, keepdims=True)
    small_a[at_plane, 1:2] = jnp.sum(bias_sum, axis=0, keepdims=True)
    small_a[at_plane, 2:3] = jnp.sum(loss, axis=0, keepdims=True)
    small_a[at_plane, 3:8] = jnp.zeros((5, C), F32)

    for n in range(1, 16):
        pltpu.make_async_remote_copy(
            small_a.at[at_plane], small_a.at[at_plane], a_send, a_recv,
            device_id=me.in_plane(0, n // 4, 2, n % 4), device_id_type=MESH,
        ).start()

    for u in range(3):
        second_phase(u)

    small_all = pltpu.make_async_remote_copy(
        small_a.at[pl.ds(0, 15)], small_a.at[pl.ds(0, 15)], a_send, a_recv,
        device_id=partner, device_id_type=MESH,
    )
    small_all.wait_recv()
    total = small_a[0]
    for f in range(1, 16):
        total = total + small_a[f]
    at_rest = me.y * 2 + core
    small_b[at_rest] = total
    for s in range(4):
        for t in range(2):
            if s + t > 0:
                to = (me.dp_x[0] + me.dp_y[s] + core + t * across, fr)
                pltpu.make_async_remote_copy(
                    small_b.at[at_rest], small_b.at[at_rest], b_send, b_recv,
                    device_id=to, device_id_type=MESH,
                ).start()

    for u in range(3, 6):
        last_phase(u)

    rest_all = pltpu.make_async_remote_copy(
        small_b.at[pl.ds(0, 7)], small_b.at[pl.ds(0, 7)], b_send, b_recv,
        device_id=partner, device_id_type=MESH,
    )
    rest_all.wait_recv()
    total = small_b[0]
    for d in range(1, 8):
        total = total + small_b[d]
    small_out[...] = total

    for u in range(3):
        last_phase(u)

    for copy in sends:
        copy.wait_send()
    small_all.wait_send()
    rest_all.wait_send()
    for m in range(8):
        hidden_pair(m).wait_send()
    pair_copy(go.at[0], go.at[1], 1).wait_send()
    pair_copy(s3_p, s3_p, 2).wait_send()
    pair_copy(gs.at[0], gs.at[1], 3).wait_send()
    for u in range(UNITS):
        first_steps(u, "send")
        plane_all(u).wait_send()


def finish(rows, small, space, time, gain, bias, loss):
    space[...] = rows[0:45]
    time[...] = rows[48:63]
    gain[...] = small[0]
    bias[...] = small[1]
    loss[0, 0] = jnp.sum(small[2:3]) / float(16 * FRAMES * ROWS * COLS * C)


def shards(clips_in, teacher, spatial_weight, temporal_weight, norm_gain, norm_bias):
    vmem = pl.BlockSpec(memory_space=pltpu.VMEM)
    hbm = pl.BlockSpec(memory_space=pl.ANY)
    dma = pltpu.SemaphoreType.DMA
    wide = [high - low for low, high in LANES]
    rows, small = pl.pallas_call(
        kernel,
        out_shape=(
            jax.ShapeDtypeStruct((64, C), F32),
            jax.ShapeDtypeStruct((8, C), F32),
        ),
        in_specs=[hbm, hbm, vmem, vmem, hbm, hbm],
        out_specs=(vmem, vmem),
        scratch_shapes=[
            pltpu.VMEM((3, 3 * C, C), BF16),
            pltpu.VMEM((3 * C, C), BF16),
            pltpu.VMEM((ROWS, COLS, C), BF16),
            pltpu.VMEM((ROWS, COLS, C), BF16),
            pltpu.VMEM((FRAMES, WIDE * ROWS, C), BF16),
            pltpu.VMEM((FRAMES, OWN * ROWS, C), BF16),
            pltpu.VMEM((FRAMES, WIDE * ROWS, C), BF16),
            pltpu.VMEM((FRAMES, OWN * ROWS, C), BF16),
            pltpu.VMEM((FRAMES, 16, C), F32),
            pltpu.VMEM((CELLS_WIDE, 3 * C), BF16),
            pltpu.VMEM((9 * C + 48, CELLS), BF16),
            pltpu.VMEM((8, 384, CELLS), BF16),
            pltpu.VMEM((CELLS, 3 * C), BF16),
            pltpu.VMEM((3 * C + 16, CELLS), BF16),
            pltpu.VMEM((8, 144, CELLS), BF16),
            pltpu.VMEM((2, CELLS, C), BF16),
            pltpu.VMEM((2, CELLS, C), BF16),
            pltpu.VMEM((CELLS_WIDE, C), BF16),
            pltpu.VMEM((TILES, CELLS_WIDE, 128), F32),
            *[pltpu.VMEM((8, 8, BLOCK, n), BF16) for n in wide],
            *[pltpu.VMEM((3, 16, BLOCK, n), BF16) for n in wide],
            *[pltpu.VMEM((16, BLOCK, n), BF16) for n in wide],
            *[pltpu.VMEM((15, BLOCK, n), BF16) for n in wide],
            pltpu.VMEM((16, 8, C), F32),
            pltpu.VMEM((8, 8, C), F32),
            dma((10,)),
            dma((2,)),
            dma((8,)), dma((8,)),
            dma((8,)), dma((8,)),
            dma((8,)), dma((8,)),
            dma((4,)), dma((4,)),
            dma((8,)), dma((8,)),
            dma((UNITS, 3)), dma((UNITS, 3)),
            dma((UNITS,)), dma((UNITS,)),
            dma, dma,
            dma, dma,
        ],
        compiler_params=pltpu.CompilerParams(
            collective_id=0, has_side_effects=True, vmem_limit_bytes=64 * 2**20 - 2**17
        ),
    )(
        clips_in.reshape(ROWS, COLS, C), teacher.reshape(ROWS, COLS, C), norm_gain, norm_bias,
        spatial_weight, temporal_weight.reshape(3 * C, C),
    )
    spatial_grad, temporal_grad, gain_grad, bias_grad, loss = pl.pallas_call(
        finish,
        out_shape=(
            jax.ShapeDtypeStruct((45, C), F32),
            jax.ShapeDtypeStruct((15, C), F32),
            jax.ShapeDtypeStruct((C,), F32),
            jax.ShapeDtypeStruct((C,), F32),
            jax.ShapeDtypeStruct((1, 1), F32),
        ),
        in_specs=[vmem, vmem],
        out_specs=(vmem, vmem, vmem, vmem, pl.BlockSpec(memory_space=pltpu.SMEM)),
    )(rows, small)
    return (spatial_grad, temporal_grad, gain_grad, bias_grad, loss.reshape(()))


def solution(mesh):
    return jax.shard_map(
        shards,
        mesh=mesh,
        in_specs=(
            P("dp", "frame", None, None, None),
            P("dp", "frame", None, None, None),
            P(),
            P(),
            P(),
            P(),
        ),
        out_specs=(P(("dp", "frame"), None), P(("dp", "frame"), None), P(), P(), P()),
        check_vma=False,
    )
```

```python
import jax
import jax.numpy as jnp
from jax import lax
from jax.experimental import pallas as pl
from jax.experimental.pallas import tpu as pltpu
from jax.sharding import PartitionSpec as P

GROUPS = 32
EPSILON = 1e-05
F32 = jnp.float32
BF16 = jnp.bfloat16
MESH = pl.DeviceIdType.MESH

FRAMES = 8
ROWS = 8
COLS = 96
C = 640
OWN = COLS // FRAMES
WIDE = OWN + 2
CELLS = OWN * FRAMES * ROWS
CELLS_WIDE = WIDE * FRAMES * ROWS
SLAB = FRAMES * ROWS
BLOCK = 16
TILES = C // 128
AXES = ((2, 0, 1), (1, 2, 0), (0, 1, 2), (0, 1, 2), (1, 2, 0), (2, 0, 1))
LANES = ((0, C), (0, C), (0, C), (0, 256), (256, 512), (512, C))
UNITS = 6


def rem(a, b):
    return lax.rem(a, jnp.int32(b))


def div(a, b):
    return lax.div(a, jnp.int32(b))


class Place:
    def __init__(self):
        self.dp = lax.axis_index("dp")
        self.fr = lax.axis_index("frame")
        self.core = rem(self.dp, 2)
        self.y = rem(div(self.dp, 2), 4)
        self.xh = div(self.dp, 8)
        self.z = div(self.fr, 2)
        self.xl = rem(self.fr, 2)
        self.x = 2 * self.xh + self.xl
        self.group = self.xh * 4 + self.y
        self.along = (self.x, self.y, self.z)

        self.at = [[rem(v + step, 4) for step in range(4)] for v in self.along]
        self.dp_x = [div(v, 2) * 8 for v in self.at[0]]
        self.fr_x = [rem(v, 2) for v in self.at[0]]
        self.dp_y = [2 * v for v in self.at[1]]
        self.fr_z = [2 * v for v in self.at[2]]

    def further(self, *steps):
        x, y, z = steps
        return (self.dp_x[x] + self.dp_y[y] + self.core, self.fr_z[z] + self.fr_x[x])

    def nth_group(self, n):
        k = rem(n, 4)
        step = jnp.where(k == 0, 2, jnp.where(k == 1, 1, jnp.where(k == 2, 3, 0)))
        half = jnp.where(n < 4, 1 - self.xh, self.xh)
        return half * 4 + rem(self.y + step, 4)

    def along_axis(self, axis, step):
        return self.further(*(step if axis == n else 0 for n in range(3)))

    def in_plane(self, one, step_one, two, step_two):
        return self.further(
            *(step_one if n == one else step_two if n == two else 0 for n in range(3))
        )


def kernel(
    x_hbm, t_hbm, gain_ref, bias_ref, w_hbm, wt_hbm,
    rows_out, small_out,
    w, wt, wtt, xraw, traw, xs, ts, xr, tr, stats, hid, hid_t, hid_p, s3, s3_t, s3_p, go, gs, xj, acc,
    stage0, stage1, stage2, stage3, stage4, stage5,
    r10, r11, r12, r13, r14, r15,
    p20, p21, p22, p23, p24, p25,
    r20, r21, r22, r23, r24, r25,
    small_a, small_b,
    w_sem, own_sem, x_send, x_recv, t_send, t_recv, st_send, st_recv, pair_send, pair_recv,
    hp_send, hp_recv, r1_send, r1_recv, r2_send, r2_recv, a_send, a_recv, b_send, b_recv,
):
    me = Place()
    dp, fr, core = me.dp, me.fr, me.core
    gs3 = s3
    g3 = hid
    stage = (stage0, stage1, stage2, stage3, stage4, stage5)
    r1 = (r10, r11, r12, r13, r14, r15)
    p2 = (p20, p21, p22, p23, p24, p25)
    r2 = (r20, r21, r22, r23, r24, r25)

    def get(at):
        return jnp.concatenate([acc[l, at, :] for l in range(TILES)], axis=1)

    def put(at, value):
        for l in range(TILES):
            acc[l, at, :] = value[:, l * 128 : (l + 1) * 128]

    load_x = pltpu.make_async_copy(x_hbm, xraw, own_sem.at[0])
    load_x.start()
    load_t = pltpu.make_async_copy(t_hbm, traw, own_sem.at[1])
    load_t.start()

    w_copies = []
    for a in range(3):
        for c in range(3):
            w_copies.append(
                pltpu.make_async_copy(
                    w_hbm.at[a, c], w.at[c, pl.ds(a * C, C)], w_sem.at[3 * a + c]
                )
            )
    w_copies.append(pltpu.make_async_copy(wt_hbm, wt, w_sem.at[9]))
    for copy in w_copies:
        copy.start()

    barrier = pltpu.get_barrier_semaphore()

    def greet(device):
        pl.semaphore_signal(barrier, inc=1, device_id=device, device_id_type=MESH)

    for axis in range(3):
        for s in range(1, 4):
            greet(me.along_axis(axis, s))
    for one, two in ((0, 1), (1, 2), (0, 2)):
        for s in range(1, 4):
            for t in range(1, 4):
                greet(me.in_plane(one, s, two, t))
    across = 1 - 2 * core
    for s in range(4):
        greet((me.dp_x[0] + me.dp_y[s] + core + across, fr))
    partner = (dp + across, fr)

    load_x.wait()

    def moment_body(i, carry):
        total, square = carry
        v = xraw[i].astype(F32)
        put(pl.ds(pl.multiple_of(i * COLS, 8), COLS), v)
        v = v.reshape(COLS // 8, 8, C)
        return (total + jnp.sum(v, axis=0), square + jnp.sum(v * v, axis=0))

    zero = jnp.zeros((8, C), F32)
    total, square = lax.fori_loop(0, ROWS, moment_body, (zero, zero))
    stats[fr, 0:8] = total
    stats[fr, 8:16] = square

    pl.semaphore_wait(barrier, 40)

    sends = []
    for s in range(1, 8):
        to = rem(fr + s, 8)
        copy = pltpu.make_async_remote_copy(
            stats.at[fr], stats.at[fr], st_send.at[s], st_recv.at[s],
            device_id=(dp, to), device_id_type=MESH,
        )
        copy.start()
        sends.append(copy)

    def two_columns(first, second):
        return jnp.concatenate(
            [
                jnp.concatenate(
                    [acc[l, pl.ds(j, ROWS, stride=COLS), :] for l in range(TILES)], axis=1
                )
                for j in (first, second)
            ],
            axis=0,
        ).astype(BF16)

    def x_share(ref, to):
        def body(jj, carry):
            j = OWN * to - 1 + 2 * jj
            ref[pl.ds(pl.multiple_of(16 * jj, 16), 16), :] = two_columns(
                jnp.maximum(j, 0), jnp.minimum(j + 1, COLS - 1)
            )
            return carry

        lax.fori_loop(0, WIDE // 2, body, 0)

    def t_share(ref, to):
        def body(jj, carry):
            j = OWN * to + 2 * jj
            ref[pl.ds(pl.multiple_of(16 * jj, 16), 16), :] = two_columns(j, j + 1)
            return carry

        lax.fori_loop(0, OWN // 2, body, 0)

    for s in range(1, 8):
        to = rem(fr + s, 8)
        x_share(xs.at[s], to)
        copy = pltpu.make_async_remote_copy(
            xs.at[s], xr.at[fr], x_send.at[s], x_recv.at[s],
            device_id=(dp, to), device_id_type=MESH,
        )
        copy.start()
        sends.append(copy)
    x_share(xr.at[fr], fr)

    load_t.wait()

    def teacher_body(i, carry):
        put(pl.ds(pl.multiple_of(i * COLS, 8), COLS), traw[i].astype(F32))
        return carry

    lax.fori_loop(0, ROWS, teacher_body, 0)
    for s in range(1, 8):
        to = rem(fr + s, 8)
        t_share(ts.at[s], to)
    t_share(tr.at[fr], fr)

    hid_t[9 * C :, :] = jnp.zeros((48, CELLS), BF16)
    s3_t[3 * C :, :] = jnp.zeros((16, CELLS), BF16)

    w_copies.pop().wait()
    for t in range(3):
        wtt[t * C : (t + 1) * C, :] = wt[t * C : (t + 1) * C, :].T

    row = lax.broadcasted_iota(jnp.int32, (C, C), 0)
    col = lax.broadcasted_iota(jnp.int32, (C, C), 1)
    same = (
        lax.shift_right_logical(row * 3277, 16) == lax.shift_right_logical(col * 3277, 16)
    ).astype(F32).astype(BF16)
    for s in range(1, 8):
        sender = rem(fr - s + 8, 8)
        pltpu.make_async_remote_copy(
            stats.at[sender], stats.at[sender], st_send.at[s], st_recv.at[s],
            device_id=(dp, sender), device_id_type=MESH,
        ).wait_recv()
    moments = stats[0]
    for f in range(1, FRAMES):
        moments = moments + stats[f]
    high = moments.astype(BF16)
    rest = moments - high.astype(F32)
    middle = rest.astype(BF16)
    low = (rest - middle.astype(F32)).astype(BF16)
    wide = (
        jnp.dot(high, same, preferred_element_type=F32)
        + jnp.dot(middle, same, preferred_element_type=F32)
        + jnp.dot(low, same, preferred_element_type=F32)
    )
    size = float(FRAMES * ROWS * COLS * (C // GROUPS))
    mean = jnp.sum(wide[0:8], axis=0, keepdims=True) / size
    variance = jnp.sum(wide[8:16], axis=0, keepdims=True) / size - mean * mean
    inverse = lax.rsqrt(variance + EPSILON)
    gain = gain_ref[...].reshape(1, C)
    bias = bias_ref[...].reshape(1, C)

    for s in range(1, 8):
        sender = rem(fr - s + 8, 8)
        pltpu.make_async_remote_copy(
            xr.at[sender], xr.at[sender], x_send.at[s], x_recv.at[s],
            device_id=(dp, sender), device_id_type=MESH,
        ).wait_recv()
        copy = pltpu.make_async_remote_copy(
            ts.at[s], tr.at[fr], t_send.at[s], t_recv.at[s],
            device_id=(dp, rem(fr + s, 8)), device_id_type=MESH,
        )
        copy.start()
        sends.append(copy)

    cell_row = rem(lax.broadcasted_iota(jnp.int32, (BLOCK, C), 0), 8)

    def valid_of(j):
        outside = ((j == 0) & (fr == 0)) | ((j == WIDE - 1) & (fr == FRAMES - 1))
        return 1.0 - outside.astype(F32)

    def sigmoid(v):
        return 0.5 * jnp.tanh(0.5 * v) + 0.5

    def store_row_shifts(ref, at, value, first, last):
        ref[at, first * C : (first + 1) * C] = jnp.where(
            cell_row == 0, 0.0, pltpu.roll(value, 1, 0)
        ).astype(BF16)
        ref[at, C : 2 * C] = value.astype(BF16)
        ref[at, last * C : (last + 1) * C] = jnp.where(
            cell_row == 7, 0.0, pltpu.roll(value, BLOCK - 1, 0)
        ).astype(BF16)

    def hidden_body(n, carry):
        p = div(n, WIDE // 2)
        jj = rem(n, WIDE // 2)
        at = pl.ds(pl.multiple_of(jj * 16, 16), 16)
        even = xr[2 * p, at].astype(F32)
        odd = xr[2 * p + 1, at].astype(F32)
        for h in range(2):
            j = 2 * jj + h
            v = jnp.concatenate([even[8 * h : 8 * h + 8], odd[8 * h : 8 * h + 8]], axis=0)
            normed = (v - mean) * inverse * gain + bias
            value = normed * sigmoid(normed) * valid_of(j)
            dst = pl.ds(pl.multiple_of(j * SLAB + p * 16, 16), 16)
            xj[dst, :] = v.astype(BF16)
            store_row_shifts(hid, dst, value, 0, 2)
        return carry

    lax.fori_loop(0, 4 * (WIDE // 2), hidden_body, 0)

    def pair_copy(src, dst, n):
        return pltpu.make_async_remote_copy(
            src, dst, pair_send.at[n], pair_recv.at[n], device_id=partner, device_id_type=MESH
        )

    pad8 = jnp.zeros((8, C), F32)

    def store_frame_shifts(ref, at, value, before, after):
        ref[at, before * C : (before + 1) * C] = jnp.concatenate(
            [pad8, value[: SLAB - 8]], axis=0
        ).astype(BF16)
        ref[at, C : 2 * C] = value.astype(BF16)
        ref[at, after * C : (after + 1) * C] = jnp.concatenate(
            [value[8:], pad8], axis=0
        ).astype(BF16)

    def rows_of(b):
        return pl.ds(pl.multiple_of(b * 256, 256), 256)

    def hidden_pair(m, lanes=pl.ds(0, CELLS)):
        src = pl.ds(pl.multiple_of(720 * m + 352 * (1 - core), 16), 384)
        return pltpu.make_async_remote_copy(
            hid_t.at[src, lanes], hid_p.at[m, :, lanes], hp_send.at[m], hp_recv.at[m],
            device_id=partner, device_id_type=MESH,
        )

    for copy in w_copies:
        copy.wait()

    def forward_body(b, carry):
        windows = [
            hid[pl.ds(pl.multiple_of(b * 256 + c * SLAB, 64), 256), :] for c in range(3)
        ]
        total = jnp.dot(
            jnp.concatenate(windows, axis=1), w[...].reshape(9 * C, C),
            preferred_element_type=F32,
        )
        for c in range(3):
            for a in range(3):
                top = (a * 3 + c) * C
                for half in range(2):
                    src = pl.ds(pl.multiple_of(b * 256 + c * SLAB + half * 128, 64), 128)
                    dst = pl.ds(pl.multiple_of(b * 256 + half * 128, 128), 128)
                    hid_t[top : top + C, dst] = hid[src, a * C : (a + 1) * C].T

        def hidden_send(n, carry):
            hidden_pair(me.nth_group(n), rows_of(b)).start()
            return carry

        lax.fori_loop(0, 8, hidden_send, 0)
        for k in range(4):
            at = pl.ds(pl.multiple_of(b * 256 + k * SLAB, SLAB), SLAB)
            store_frame_shifts(s3, at, total[k * SLAB : (k + 1) * SLAB], 0, 2)
        put(rows_of(b), jnp.dot(s3[rows_of(b), :], wt[...], preferred_element_type=F32))
        for t in range(3):
            for half in range(2):
                at = pl.ds(pl.multiple_of(b * 256 + half * 128, 128), 128)
                s3_t[t * C : (t + 1) * C, at] = s3[at, t * C : (t + 1) * C].T
        for m in range(8):
            src = pl.ds(pl.multiple_of(240 * m + 112 * (1 - core), 16), 144)
            pair_copy(s3_t.at[src, rows_of(b)], s3_p.at[m, :, rows_of(b)], 2).start()
        return carry

    lax.fori_loop(0, 3, forward_body, 0)

    for s in range(1, 8):
        sender = rem(fr - s + 8, 8)
        pltpu.make_async_remote_copy(
            tr.at[sender], tr.at[sender], t_send.at[s], t_recv.at[s],
            device_id=(dp, sender), device_id_type=MESH,
        ).wait_recv()

    scale = float(16 * FRAMES * ROWS * COLS) ** (-0.5)

    def nt(lhs, rhs):
        return lax.dot_general(lhs, rhs, (((1,), (1,)), ((), ())), preferred_element_type=F32)

    def backward_body(b, loss):
        for half in range(2):
            jj = 2 * b + half
            at = pl.ds(pl.multiple_of(jj * 16, 16), 16)
            target = [tr[f, at].astype(F32) for f in range(FRAMES)]
            for h in range(2):
                j = 2 * jj + h
                own = pl.ds(pl.multiple_of(j * SLAB, SLAB), SLAB)
                wide_at = pl.ds(pl.multiple_of((j + 1) * SLAB, SLAB), SLAB)
                taught = jnp.concatenate([t[8 * h : 8 * h + 8] for t in target], axis=0)
                out = get(own).astype(BF16).astype(F32)
                error = xj[wide_at, :].astype(F32) + out - taught
                grad = error * scale
                go[0, own, :] = grad.astype(BF16)
                store_frame_shifts(g3, own, grad, 2, 0)
                loss = loss + jnp.sum((error * error).reshape(FRAMES, 8, C), axis=0)
        src = rows_of(b)
        pair_copy(go.at[0, src], go.at[1, src], 1).start()
        total = jnp.dot(g3[src, :], wtt[...], preferred_element_type=F32)
        for k in range(16):
            at = pl.ds(pl.multiple_of(b * 256 + 16 * k, 16), 16)
            value = total[16 * k : 16 * k + 16]
            gs[0, at, :] = value.astype(BF16)
            store_row_shifts(gs3, at, value, 2, 0)
        pair_copy(gs.at[0, src], gs.at[1, src], 3).start()
        return loss

    loss = lax.fori_loop(0, 3, backward_body, jnp.zeros((8, C), F32))

    def wait_pair(dst, n):
        pair_copy(dst, dst, n).wait_recv()

    wait_pair(go.at[1], 1)
    wait_pair(s3_p, 2)

    def time_body(n, carry):
        own = jnp.concatenate(
            [
                s3_t[pl.ds(pl.multiple_of(240 * (4 * n + k) + 112 * core, 16), 144), :]
                for k in range(4)
            ],
            axis=0,
        )
        other = s3_p[pl.ds(4 * n, 4)].reshape(576, CELLS)
        both = jnp.concatenate([own, other], axis=1)
        out = jnp.dot(both, go[...].reshape(2 * CELLS, C), preferred_element_type=F32)
        put(pl.ds(0, 576), out)
        for k in range(4):
            for q in range(8):
                cut = 15 * q % 8
                at = pl.ds(pl.multiple_of(144 * k + 15 * q - cut + 8 * core, 8), 24)
                rows = get(at)[cut : cut + 16].astype(BF16)
                zz, xl = q // 2, q % 2
                stage[3][4 * n + k, xl * 4 + zz] = rows[:, 0:256]
                stage[4][4 * n + k, q] = rows[:, 256:512]
                stage[5][4 * n + k, q] = rows[:, 512:C]
        return carry

    lax.fori_loop(0, 2, time_body, 0)

    def first_send(u, src, step, dst, device):
        pltpu.make_async_remote_copy(
            src, dst, r1_send.at[u, step - 1], r1_recv.at[u, step - 1],
            device_id=device, device_id_type=MESH,
        ).start()

    def send_y(u, m):
        mx, my = div(m, 4), rem(m, 4)
        step = rem(my - me.y + 4, 4)

        @pl.when(step != 0)
        def _():
            first_send(
                u, stage[u].at[m], step,
                r1[u].at[step - 1, pl.ds(mx * 8, 8)],
                (me.dp_x[0] + 2 * my + core, fr),
            )

    def send_z(u, m):
        for s in range(1, 4):
            first_send(
                u, stage[u].at[m, pl.ds(me.fr_z[s], 2)], s,
                r1[u].at[s - 1, pl.ds(m * 2, 2)], me.along_axis(2, s),
            )

    def send_x(u, m):
        mx, my = div(m, 4), rem(m, 4)
        for xl in range(2):
            there = 2 * mx + xl
            step = rem(there - me.x + 4, 4)

            @pl.when(step != 0)
            def _():
                first_send(
                    u, stage[u].at[m, pl.ds(xl * 4, 4)], step,
                    r1[u].at[step - 1, pl.ds(my * 4, 4)],
                    (mx * 8 + me.dp_y[0] + core, me.fr_z[0] + xl),
                )

    for step in range(1, 4):
        there = pl.ds(div(me.dp_x[step], 2), 4), pl.ds(me.fr_x[step] * 4, 4)
        first_send(3, stage[3].at[there], step, r1[3].at[step - 1], me.along_axis(0, step))
        for mx in range(2):
            first_send(
                4, stage[4].at[mx * 4 + me.at[1][step]], step,
                r1[4].at[step - 1, pl.ds(mx * 8, 8)], me.along_axis(1, step),
            )
        there = pl.ds(0, 8), pl.ds(me.fr_z[step], 2)
        first_send(5, stage[5].at[there], step, r1[5].at[step - 1], me.along_axis(2, step))

    wait_pair(gs.at[1], 3)

    def space_cut(n):
        m = me.nth_group(n)
        half = rem(n, 2) * 384 + 8 * core
        for q in range(8):
            cut = 45 * q % 8
            at = pl.ds(pl.multiple_of(half + 45 * q - cut, 8), 56)
            rows = get(at)[cut : cut + 48].astype(BF16)
            zz, xl = q // 2, q % 2
            stage[0][m, q] = rows[0:16]
            stage[1][m, q] = rows[16:32]
            stage[2][m, xl * 4 + zz] = rows[32:48]

    def space_send(n):
        m = me.nth_group(n)
        send_z(0, m)
        send_y(1, m)
        send_x(2, m)

    def space_dot(n):
        m = me.nth_group(n)
        own = hid_t[pl.ds(pl.multiple_of(720 * m + 352 * core, 16), 384), :]
        both = jnp.concatenate([own, hid_p[m]], axis=1)
        out = jnp.dot(both, gs[...].reshape(2 * CELLS, C), preferred_element_type=F32)
        put(pl.ds(pl.multiple_of(rem(n, 2) * 384, 128), 384), out)

    hidden_pair(me.nth_group(jnp.int32(0))).wait_recv()
    space_dot(jnp.int32(0))

    def space_body(n, carry):
        hidden_pair(me.nth_group(n)).wait_recv()
        space_cut(n - 1)
        space_dot(n)
        space_send(n - 1)
        return carry

    lax.fori_loop(1, 8, space_body, 0)
    space_cut(jnp.int32(7))
    space_send(jnp.int32(7))

    put(pl.ds(CELLS, 2 * SLAB), jnp.zeros((2 * SLAB, C), F32))

    def grad_hidden(c):
        def body(b, carry):
            src = pl.ds(pl.multiple_of(b * 256, 256), 256)
            dst = pl.ds(pl.multiple_of(b * 256 + c * SLAB, 64), 256)
            total = get(dst) if c > 0 else None
            for a in range(3):
                part = nt(gs3[src, a * C : (a + 1) * C], w[c, a * C : (a + 1) * C, :])
                total = part if total is None else total + part
            put(dst, total)
            return carry

        lax.fori_loop(0, 3, body, 0)

    def first_steps(u, wait):
        for s in range(1, 4):
            copy = pltpu.make_async_remote_copy(
                r1[u].at[s - 1], r1[u].at[s - 1], r1_send.at[u, s - 1], r1_recv.at[u, s - 1],
                device_id=me.along_axis(0, 1), device_id_type=MESH,
            )
            if wait == "recv":
                copy.wait_recv()
            else:
                copy.wait_send()

    def plane_copy(u, src, dst, device):
        return pltpu.make_async_remote_copy(
            src, dst, r2_send.at[u], r2_recv.at[u], device_id=device, device_id_type=MESH
        )

    def plane_all(u):
        return plane_copy(u, r2[u], r2[u], me.along_axis(0, 1))

    def second_phase(u):
        first_steps(u, "recv")
        axis, one, two = AXES[u]
        for step_one in range(4):
            for step_two in range(4):
                n = step_one * 4 + step_two
                if axis == 2:
                    x_half, xl, y = div(me.dp_x[step_one], 8), me.fr_x[step_one], me.at[1][step_two]
                    k = x_half * 8 + y * 2 + xl
                    own = stage[u][x_half * 4 + y, me.fr_z[0] + xl]
                elif axis == 0:
                    y, z = me.at[1][step_one], me.at[2][step_two]
                    k = y * 4 + z
                    own = stage[u][me.xh * 4 + y, me.xl * 4 + z]
                else:
                    q = me.fr_z[step_one] + me.fr_x[step_two]
                    k = me.dp_x[step_two] + q
                    own = stage[u][div(me.dp_x[step_two], 2) + me.y, q]
                if u == 3:
                    k = (y, z)
                elif u == 5:
                    k = (x_half * 4 + y, xl)
                else:
                    k = (k,)
                total = own.astype(F32)
                for s in range(3):
                    total = total + r1[u][(s, *k)].astype(F32)
                p2[u][n] = total.astype(BF16)
                if n > 0:
                    plane_copy(
                        u, p2[u].at[n], r2[u].at[n - 1],
                        me.in_plane(one, step_one, two, step_two),
                    ).start()

    def last_phase(u):
        plane_all(u).wait_recv()
        total = p2[u][0].astype(F32)
        for n in range(15):
            total = total + r2[u][n].astype(F32)
        low, high = LANES[u]
        top = min(u, 3) * BLOCK
        rows_out[top : top + BLOCK, low:high] = total

    grad_hidden(0)
    for u in range(3, 6):
        second_phase(u)
    grad_hidden(1)
    grad_hidden(2)

    def norm_body(n, carry):
        gain_sum, bias_sum = carry
        at = pl.ds(pl.multiple_of(n * 16, 16), 16)
        centred = (xj[at, :].astype(F32) - mean) * inverse
        normed = centred * gain + bias
        s = sigmoid(normed)
        grad = get(at) * s * (1.0 + normed * (1.0 - s)) * valid_of(div(n, 4))
        weighted = grad * centred
        return (gain_sum + weighted[0:8] + weighted[8:16], bias_sum + grad[0:8] + grad[8:16])

    gain_sum, bias_sum = lax.fori_loop(0, CELLS_WIDE // 16, norm_body, (zero, zero), unroll=2)
    at_plane = me.x * 4 + me.z
    small_a[at_plane, 0:1] = jnp.sum(gain_sum, axis=0, keepdims=True)
    small_a[at_plane, 1:2] = jnp.sum(bias_sum, axis=0, keepdims=True)
    small_a[at_plane, 2:3] = jnp.sum(loss, axis=0, keepdims=True)
    small_a[at_plane, 3:8] = jnp.zeros((5, C), F32)

    for n in range(1, 16):
        pltpu.make_async_remote_copy(
            small_a.at[at_plane], small_a.at[at_plane], a_send, a_recv,
            device_id=me.in_plane(0, n // 4, 2, n % 4), device_id_type=MESH,
        ).start()

    for u in range(3):
        second_phase(u)

    small_all = pltpu.make_async_remote_copy(
        small_a.at[pl.ds(0, 15)], small_a.at[pl.ds(0, 15)], a_send, a_recv,
        device_id=partner, device_id_type=MESH,
    )
    small_all.wait_recv()
    total = small_a[0]
    for f in range(1, 16):
        total = total + small_a[f]
    at_rest = me.y * 2 + core
    small_b[at_rest] = total
    for s in range(4):
        for t in range(2):
            if s + t > 0:
                to = (me.dp_x[0] + me.dp_y[s] + core + t * across, fr)
                pltpu.make_async_remote_copy(
                    small_b.at[at_rest], small_b.at[at_rest], b_send, b_recv,
                    device_id=to, device_id_type=MESH,
                ).start()

    for u in range(3, 6):
        last_phase(u)

    rest_all = pltpu.make_async_remote_copy(
        small_b.at[pl.ds(0, 7)], small_b.at[pl.ds(0, 7)], b_send, b_recv,
        device_id=partner, device_id_type=MESH,
    )
    rest_all.wait_recv()
    total = small_b[0]
    for d in range(1, 8):
        total = total + small_b[d]
    small_out[...] = total

    for u in range(3):
        last_phase(u)

    for copy in sends:
        copy.wait_send()
    small_all.wait_send()
    rest_all.wait_send()
    for m in range(8):
        hidden_pair(m).wait_send()
    pair_copy(go.at[0], go.at[1], 1).wait_send()
    pair_copy(s3_p, s3_p, 2).wait_send()
    pair_copy(gs.at[0], gs.at[1], 3).wait_send()
    for u in range(UNITS):
        first_steps(u, "send")
        plane_all(u).wait_send()


def finish(rows, small, space, time, gain, bias, loss):
    space[...] = rows[0:45]
    time[...] = rows[48:63]
    gain[...] = small[0]
    bias[...] = small[1]
    loss[0, 0] = jnp.sum(small[2:3]) / float(16 * FRAMES * ROWS * COLS * C)


def shards(clips_in, teacher, spatial_weight, temporal_weight, norm_gain, norm_bias):
    vmem = pl.BlockSpec(memory_space=pltpu.VMEM)
    hbm = pl.BlockSpec(memory_space=pl.ANY)
    dma = pltpu.SemaphoreType.DMA
    wide = [high - low for low, high in LANES]
    rows, small = pl.pallas_call(
        kernel,
        out_shape=(
            jax.ShapeDtypeStruct((64, C), F32),
            jax.ShapeDtypeStruct((8, C), F32),
        ),
        in_specs=[hbm, hbm, vmem, vmem, hbm, hbm],
        out_specs=(vmem, vmem),
        scratch_shapes=[
            pltpu.VMEM((3, 3 * C, C), BF16),
            pltpu.VMEM((3 * C, C), BF16),
            pltpu.VMEM((3 * C, C), BF16),
            pltpu.VMEM((ROWS, COLS, C), BF16),
            pltpu.VMEM((ROWS, COLS, C), BF16),
            pltpu.VMEM((FRAMES, WIDE * ROWS, C), BF16),
            pltpu.VMEM((FRAMES, OWN * ROWS, C), BF16),
            pltpu.VMEM((FRAMES, WIDE * ROWS, C), BF16),
            pltpu.VMEM((FRAMES, OWN * ROWS, C), BF16),
            pltpu.VMEM((FRAMES, 16, C), F32),
            pltpu.VMEM((CELLS_WIDE, 3 * C), BF16),
            pltpu.VMEM((9 * C + 48, CELLS), BF16),
            pltpu.VMEM((8, 384, CELLS), BF16),
            pltpu.VMEM((CELLS, 3 * C), BF16),
            pltpu.VMEM((3 * C + 16, CELLS), BF16),
            pltpu.VMEM((8, 144, CELLS), BF16),
            pltpu.VMEM((2, CELLS, C), BF16),
            pltpu.VMEM((2, CELLS, C), BF16),
            pltpu.VMEM((CELLS_WIDE, C), BF16),
            pltpu.VMEM((TILES, CELLS_WIDE, 128), F32),
            *[pltpu.VMEM((8, 8, BLOCK, n), BF16) for n in wide],
            *[pltpu.VMEM((3, 16, BLOCK, n), BF16) for n in wide[:3]],
            pltpu.VMEM((3, 4, 4, BLOCK, wide[3]), BF16),
            pltpu.VMEM((3, 16, BLOCK, wide[4]), BF16),
            pltpu.VMEM((3, 8, 2, BLOCK, wide[5]), BF16),
            *[pltpu.VMEM((16, BLOCK, n), BF16) for n in wide],
            *[pltpu.VMEM((15, BLOCK, n), BF16) for n in wide],
            pltpu.VMEM((16, 8, C), F32),
            pltpu.VMEM((8, 8, C), F32),
            dma((10,)),
            dma((2,)),
            dma((8,)), dma((8,)),
            dma((8,)), dma((8,)),
            dma((8,)), dma((8,)),
            dma((4,)), dma((4,)),
            dma((8,)), dma((8,)),
            dma((UNITS, 3)), dma((UNITS, 3)),
            dma((UNITS,)), dma((UNITS,)),
            dma, dma,
            dma, dma,
        ],
        compiler_params=pltpu.CompilerParams(
            collective_id=0, has_side_effects=True, vmem_limit_bytes=64 * 2**20 - 2**17
        ),
    )(
        clips_in.reshape(ROWS, COLS, C), teacher.reshape(ROWS, COLS, C), norm_gain, norm_bias,
        spatial_weight, temporal_weight.reshape(3 * C, C),
    )
    spatial_grad, temporal_grad, gain_grad, bias_grad, loss = pl.pallas_call(
        finish,
        out_shape=(
            jax.ShapeDtypeStruct((45, C), F32),
            jax.ShapeDtypeStruct((15, C), F32),
            jax.ShapeDtypeStruct((C,), F32),
            jax.ShapeDtypeStruct((C,), F32),
            jax.ShapeDtypeStruct((1, 1), F32),
        ),
        in_specs=[vmem, vmem],
        out_specs=(vmem, vmem, vmem, vmem, pl.BlockSpec(memory_space=pltpu.SMEM)),
    )(rows, small)
    return (spatial_grad, temporal_grad, gain_grad, bias_grad, loss.reshape(()))


def solution(mesh):
    return jax.shard_map(
        shards,
        mesh=mesh,
        in_specs=(
            P("dp", "frame", None, None, None),
            P("dp", "frame", None, None, None),
            P(),
            P(),
            P(),
            P(),
        ),
        out_specs=(P(("dp", "frame"), None), P(("dp", "frame"), None), P(), P(), P()),
        check_vma=False,
    )
```
